32 devices in a mesh: orb: 32 (over z, y, x, core).
Axes of the slice: x: 2, y: 2, z: 4, core: 2. Of those that a mesh axis runs over, the one named last changes fastest.
Arguments:
- orbitals: bfloat16 [128, 64, 4096], P('orb'), may hold values from -6 to 6
- pair_list: int32 [512, 2], P('orb'), may hold values from 0 to 15, as said below
- pair_counts: int32 [32], P('orb'), may hold values from 1 to 16, as said below
Outputs:
- exchange_field: float32 [128, 64, 4096], P('orb')
The draws below stay inside these ranges and needn't reach their ends.
Inputs may be any that keep to these rules, and one draw needn't show every extreme that they name: `pair_list`: in each row (a, w) of a device's block, a is one of its own 4 orbitals and w is below (4) * 4; where w < 4 both orbitals are the device's own and w >= a. The rows of one device's block are distinct. `pair_counts`: some device's count is 16; rows past a device's count are not used.
All inputs are finite; a program needn't handle non-finite values.
Results may differ from the reference program's by a relative error of at most 0.0003.
Values may be sent and summed in bfloat16 or wider, within the bound.
No kernel may reach another device: no remote copies, remote signals or barrier semaphores. Data moves between devices by JAX's collectives and lax.ppermute only.
A program may use at most 128 MiB of HBM per device.

```python
import math
import jax
import jax.numpy as jnp
import numpy as np
from jax import lax

B = 64
ORB_DEV = 4
PAIR_DEV = 16
REACH = 3
ORBITALS = 128
N_ORB = 32


def candidate_table():
    local_pairs = [(a, b) for a in range(ORB_DEV) for b in range(a, ORB_DEV)]
    ahead_pairs = [(a, ORB_DEV + k) for a in range(ORB_DEV) for k in range(REACH * ORB_DEV)]
    return np.array(local_pairs + ahead_pairs, dtype=np.int32)


def draw_pair_list(key, part):
    table = jnp.asarray(candidate_table())
    keys = jax.random.split(jax.random.fold_in(key, 11), N_ORB)
    chosen = jax.vmap(lambda k: jax.random.permutation(k, table.shape[0])[:PAIR_DEV])(keys)
    return table[chosen.reshape(-1)].astype(jnp.int32)


def draw_pair_counts(key, part):
    base = jax.random.randint(jax.random.fold_in(key, 23), (N_ORB,), 1, PAIR_DEV // 2 + 1)
    quarter = jax.random.randint(jax.random.fold_in(key, 31), (N_ORB,), 0, 4)
    chosen = jax.random.randint(jax.random.fold_in(key, 29), (), 0, N_ORB)
    filled = (quarter == 0) | (jnp.arange(N_ORB) == chosen)
    return jnp.where(filled, PAIR_DEV, base).astype(jnp.int32)


def levels(key, dims, pieces, least, largest):
    def one(axis_at, shards_of):
        draws = jax.random.uniform(jax.random.fold_in(jax.random.fold_in(key, 6), axis_at), (shards_of,), jnp.float32, least / len(pieces), largest / len(pieces))
        return jnp.repeat(jnp.exp(draws), dims[axis_at] // shards_of).reshape((-1,) + (1,) * (len(dims) - axis_at - 1))

    factor_of = one(*pieces[0])
    for cut in pieces[1:]:
        factor_of = factor_of * one(*cut)
    return factor_of


def centred(own_key, extent, width, bound, pieces=(), kind=jnp.bfloat16):
    values = jax.random.normal(own_key, extent, jnp.float32) * width
    if len(pieces) > 0:
        values = levels(own_key, extent, pieces, -0.22, 0.18) * values
    return jnp.clip(values, min=-bound, max=bound).astype(kind)


def setup_inputs(seed: int = 0) -> dict:
    key_list = jax.random.split(jax.random.key(seed), 4)
    return {
        "orbitals": centred(key_list[0], (ORBITALS, B, B * B), 1.0, 6.0, ((0, 32),)),
        "pair_list": draw_pair_list(jax.random.fold_in(key_list[3], 71), 0),
        "pair_counts": draw_pair_counts(jax.random.fold_in(key_list[3], 71), 0),
    }


screening = 0.5


def sine_table(points):
    modes = jnp.arange(points, dtype=jnp.float32) + 1.0
    return jnp.sin(math.pi * modes[:, None] * modes[None, :] / (points + 1))


def inverse_denominators(points):
    modes = jnp.arange(points, dtype=jnp.float32) + 1.0
    eigen = 4.0 * jnp.sin(math.pi * modes / (2.0 * (points + 1))) ** 2
    total = eigen[:, None, None] + eigen[None, :, None] + eigen[None, None, :] + screening
    return ((2.0 / (points + 1)) ** 3 / total).reshape(points, points * points)


def sine_cube(fields, sines):
    points = sines.shape[0]
    cube = fields.reshape(points, points, points)
    highest = lax.Precision.HIGHEST
    cube = jnp.einsum("kx,xyz->kyz", sines, cube, precision=highest)
    cube = jnp.einsum("ky,xyz->xkz", sines, cube, precision=highest)
    cube = jnp.einsum("kz,xyz->xyk", sines, cube, precision=highest)
    return cube.reshape(points, points * points)


def screened_potential(density, sines, inverse):
    return sine_cube(sine_cube(density, sines) * inverse, sines)


def reference(orbitals, pair_list, pair_counts):
    box_side = orbitals.shape[1]
    sines = sine_table(box_side)
    inverse = inverse_denominators(box_side)
    orbital_total = orbitals.shape[0]
    own_count = orbital_total // N_ORB
    fields = jnp.zeros(orbitals.shape, jnp.float32)

    def add_pair(slot_index, fields):
        device = slot_index // PAIR_DEV
        slot = slot_index % PAIR_DEV
        target = device * own_count + pair_list[slot_index, 0]
        partner = (device * own_count + pair_list[slot_index, 1]) % orbital_total

        def live_pair(fields):
            one_side = orbitals[target].astype(jnp.float32)
            other_side = orbitals[partner].astype(jnp.float32)
            potential = screened_potential(one_side * other_side, sines, inverse)
            fields = fields.at[target].add(potential * other_side)
            weight = (target != partner).astype(jnp.float32)
            return fields.at[partner].add(potential * one_side * weight)

        return lax.cond(slot < pair_counts[device], live_pair, lambda kept: kept, fields)

    fields = lax.fori_loop(0, pair_list.shape[0], add_pair, fields)
    return -fields
```

```python
import functools
import math

import jax
import jax.numpy as jnp
import numpy as np
from jax import lax
from jax.experimental import pallas as pl
from jax.experimental.pallas import tpu as pltpu
from jax.sharding import PartitionSpec as P

REACH = 3
LANES = 128
GROUP = 8
NOWHERE = 99

screening = 0.5


def routes(count):
    groups = count // GROUP

    def device(group, chip, core):
        return (group % groups) * GROUP + 2 * chip + core

    names = ("x1", "x2", "x3a", "x3b", "y1", "y2", "y3a", "y3b", "z1", "z2")
    table = {name: [] for name in names}
    for g in range(groups):
        for c in range(4):
            first = 1 if c in (0, 2) else 0
            table["x1"].append((device(g, c, first), device(g, c ^ 1, first)))
            table["x2"].append((device(g, c, 1 - first), device(g, c ^ 1, 1 - first)))
            near = 1 if c in (0, 1) else 0
            table["y1"].append((device(g, c, near), device(g, c ^ 2, 1 - near)))
            edge = 1 if c in (2, 3) else 0
            step = 1 if c in (2, 3) else -1
            table["z1"].append((device(g, c, edge), device(g + step, c, edge)))
            table["y2"].append((device(g, c, edge), device(g, c ^ 2, 1 - edge)))
        table["z2"] += [(device(g, 2, 0), device(g + 1, 2, 0)), (device(g, 1, 1), device(g - 1, 1, 1))]
        table["x3a"] += [(device(g, 0, 1), device(g, 1, 1)), (device(g, 3, 0), device(g, 2, 0))]
        table["x3b"] += [(device(g, 1, 0), device(g, 0, 0)), (device(g, 2, 1), device(g, 3, 1))]
        table["y3a"] += [(device(g, 0, 0), device(g, 2, 0)), (device(g, 3, 1), device(g, 1, 1))]
        table["y3b"] += [(device(g, 2, 0), device(g, 0, 0)), (device(g, 1, 1), device(g, 3, 1))]
    table["core"] = [(d, d ^ 1) for d in range(count)]
    for name in ("x1", "x2", "x3a", "x3b", "y3a", "y3b"):
        table[name + "s"] = [(target, target ^ 1) for _, target in table[name]]
    return table


HELD = {
    "x1": (2, 1, 6, 5),
    "x2": (3, 0, 7, 4),
    "x3": (-1, 4, 3, 8),
    "y1": (4, 6, 1, 3),
    "y2": (-3, -1, 8, 10),
    "y3": (-2, 5, 2, 9),
}
TAKER = {
    "x1": (0, 1, 0, 1),
    "x2": (1, 0, 1, 0),
    "x3": (0, 1, 0, 1),
    "y1": (1, 1, 0, 0),
    "y2": (0, 0, 1, 1),
    "y3": (0, 1, 0, 1),
}


def tables(points):
    modes = np.arange(points) + 1.0
    sines = np.sin(math.pi * np.outer(modes, modes) / (points + 1)) * math.sqrt(2.0 / (points + 1))
    high = sines.astype(jnp.bfloat16)
    low = (sines - high.astype(np.float64)).astype(jnp.bfloat16)
    high, low = high.astype(np.float32), low.astype(np.float32)
    none = np.zeros_like(high)

    def straight(t):
        return np.block([[t, none], [none, t]])

    def crossed(t):
        return np.block([[none, t], [t, none]])

    def spread(form):
        return np.block([[form(high), form(low)], [form(high), form(low)]])

    along_lines = np.stack([spread(straight), spread(crossed)]).astype(jnp.bfloat16)
    along_planes = np.concatenate([high, high, low, low], 1).astype(jnp.bfloat16)
    eigen = 4.0 * np.sin(math.pi * modes / (2.0 * (points + 1))) ** 2
    diagonal = 2.0 + eigen[:, None] + eigen[None, :] + screening
    ratios = [1.0 / diagonal]
    for _ in range(points // 2 - 1):
        ratios.append(1.0 / (diagonal - ratios[-1]))
    middle = 1.0 / (1.0 - ratios[-1] ** 2)
    ratios = np.stack(ratios)
    ratios = np.concatenate([ratios, ratios], 2).astype(np.float32)
    middle = np.concatenate([middle, middle], 1).astype(np.float32)
    return along_lines, along_planes, ratios, middle


def split(value):
    high = value.astype(jnp.bfloat16)
    return high, (value - high.astype(jnp.float32)).astype(jnp.bfloat16)


def dot(left, right):
    return jnp.dot(left, right, preferred_element_type=jnp.float32)


def sine_lines(value, weights):
    product = dot(jnp.concatenate(split(value), 1), weights)
    return product[:, :LANES] + product[:, LANES:]


def sine_planes(value, weights):
    high, low = split(value)
    return dot(weights, jnp.concatenate([high, low, high, low], 0))


def tile(index):
    if isinstance(index, int):
        return pl.ds(index * LANES, LANES)
    return pl.ds(pl.multiple_of(index * LANES, LANES), LANES)


def potential_tiles(load_left, load_right, give, lines_ref, planes_ref, ratios_ref, middle_ref, kept, points):
    couples = points // 4
    last = 2 * couples - 1
    first_half = lax.broadcasted_iota(jnp.int32, (points, LANES), 1) < points
    even, odd = [], []
    for i in range(couples):
        near = load_left(i).astype(jnp.float32) * load_right(i).astype(jnp.float32)
        far = load_left(last - i).astype(jnp.float32) * load_right(last - i).astype(jnp.float32)
        even.append(jnp.where(first_half, near, far))
        odd.append(jnp.where(first_half, far, near))
    even = sine_lines(jnp.concatenate(even, 0), lines_ref[0])
    odd = sine_lines(jnp.concatenate(odd, 0), lines_ref[1])
    swept = jnp.zeros((points, LANES), jnp.float32)
    for i in range(couples):
        rows = slice(i * points, (i + 1) * points)
        modes = sine_planes(jnp.concatenate([even[rows], odd[rows]], 1), planes_ref[...])
        swept = (modes[:, :LANES] + swept) * ratios_ref[2 * i]
        kept[2 * i] = swept
        swept = (modes[:, LANES:] + swept) * ratios_ref[2 * i + 1]
        if i < couples - 1:
            kept[2 * i + 1] = swept
    solved = (swept + ratios_ref[last] * pltpu.roll(swept, points, 1)) * middle_ref[...]
    even, odd = [], []
    for i in reversed(range(couples)):
        if i < couples - 1:
            solved = kept[2 * i + 1] + ratios_ref[2 * i + 1] * solved
        later = solved
        solved = kept[2 * i] + ratios_ref[2 * i] * later
        grid = sine_planes(jnp.concatenate([solved, later], 1), planes_ref[...])
        even.append(grid[:, :LANES])
        odd.append(grid[:, LANES:])
    even = sine_lines(jnp.concatenate(even, 0), lines_ref[0])
    odd = sine_lines(jnp.concatenate(odd, 0), lines_ref[1])
    for place, i in enumerate(reversed(range(couples))):
        rows = slice(place * points, (place + 1) * points)
        give(i, jnp.where(first_half, even[rows], odd[rows]))
        give(last - i, jnp.where(first_half, odd[rows], even[rows]))


def visit_kernel(choices, fresh, with_own, points, *refs):
    refs = list(refs)
    places_ref, lists_ref, own_ref = refs[:3]
    sources, at = [], 3
    for count in choices:
        sources.append(refs[at : at + count])
        at += count
    if not fresh:
        before_ref = refs[at]
        at += 1
    lines_ref, planes_ref, ratios_ref, middle_ref, totals, window, kept, extra, items, sems = refs[at:]
    own_count = own_ref.shape[0]
    slots = lists_ref.shape[1] - 1
    blocks = len(choices)

    def brought(slot, source):
        return pltpu.make_async_copy(source, window.at[pl.ds((slot + 1) * own_count, own_count)], sems.at[slot + 1])

    own_copy = pltpu.make_async_copy(own_ref, window.at[pl.ds(0, own_count)], sems.at[0])
    own_copy.start()
    for slot in range(blocks):
        for choice, source in enumerate(sources[slot]):
            if len(sources[slot]) == 1:
                brought(slot, source).start()
            else:
                @pl.when(places_ref[slot, 1] == choice)
                def _():
                    brought(slot, source).start()
    if fresh:
        totals[...] = jnp.zeros_like(totals)
    else:
        before = pltpu.make_async_copy(before_ref, totals, sems.at[blocks + 1])
        before.start()

    def note(keep, filled, own, other):
        @pl.when(keep)
        def _():
            items[filled, 0] = own
            items[filled, 1] = other

        return filled + keep.astype(jnp.int32)

    filled = jnp.int32(0)
    if with_own:
        def add_own(row, filled):
            keep = (row < lists_ref[0, slots, 0]) & (lists_ref[0, row, 1] < own_count)
            return note(keep, filled, lists_ref[0, row, 0], lists_ref[0, row, 1])

        filled = lax.fori_loop(0, slots, add_own, filled)
    for slot in range(blocks):
        offset = places_ref[slot, 0]
        start = (slot + 1) * own_count
        ahead = offset > 0
        which = jnp.where(ahead, 0, jnp.minimum(-offset, REACH))
        distance = jnp.abs(offset)

        def add_block(row, filled):
            keep = (row < lists_ref[which, slots, 0]) & (lists_ref[which, row, 1] // own_count == distance)
            lead = lists_ref[which, row, 0]
            follow = lists_ref[which, row, 1] - distance * own_count
            return note(keep, filled, jnp.where(ahead, lead, follow), start + jnp.where(ahead, follow, lead))

        filled = lax.fori_loop(0, slots, add_block, filled)

    own_copy.wait()
    for slot in range(blocks):
        brought(slot, sources[slot][0]).wait()
    if not fresh:
        before.wait()

    def visit(item, carried):
        mine = items[item, 0]
        other = items[item, 1]

        def load_mine(index):
            return window[mine, :, tile(index)]

        def load_other(index):
            return window[other, :, tile(index)]

        def give(index, potential):
            totals[mine, :, tile(index)] -= potential * load_other(index).astype(jnp.float32)
            if with_own:
                extra[:, tile(index)] = potential

        potential_tiles(
            load_mine, load_other, give, lines_ref, planes_ref, ratios_ref, middle_ref, kept, points
        )
        if with_own:
            @pl.when((other < own_count) & (other != mine))
            def _():
                def give_back(index, carried):
                    totals[other, :, tile(index)] -= extra[:, tile(index)] * load_mine(index).astype(jnp.float32)
                    return carried

                lax.fori_loop(0, points // 2, give_back, 0)

        return carried

    lax.fori_loop(0, filled, visit, 0)


def visit_blocks(places, lists, own, sources, before, constants, with_own):
    own_count, points, area = own.shape
    choices = tuple(len(source) for source in sources)
    flat = [array for source in sources for array in source]
    blocks = len(choices)
    vmem = pl.BlockSpec(memory_space=pltpu.VMEM)
    smem = pl.BlockSpec(memory_space=pltpu.SMEM)
    hbm = pl.BlockSpec(memory_space=pl.ANY)
    fresh = before is None
    most = (lists.shape[1] - 1) * (blocks + 1)
    pairs = 5
    return pl.pallas_call(
        functools.partial(visit_kernel, choices, fresh, with_own, points),
        out_shape=jax.ShapeDtypeStruct(own.shape, jnp.float32),
        in_specs=[smem, smem, hbm] + [hbm] * len(flat) + ([] if fresh else [hbm]) + [vmem] * len(constants),
        out_specs=vmem,
        scratch_shapes=[
            pltpu.VMEM(((blocks + 1) * own_count, points, area), jnp.bfloat16),
            pltpu.VMEM((points // 2, points, LANES), jnp.float32),
            pltpu.VMEM((points, area) if with_own else (8, LANES), jnp.float32),
            pltpu.SMEM((most, 2), jnp.int32),
            pltpu.SemaphoreType.DMA((blocks + 2,)),
        ],
        compiler_params=pltpu.CompilerParams(vmem_limit_bytes=48 * 2**20),
        cost_estimate=pl.CostEstimate(
            flops=pairs * 8 * points * points * points * points * 8, bytes_accessed=16 * 2**20, transcendentals=0
        ),
    )(places, lists, own, *flat, *([] if fresh else [before]), *constants)


def shards(orbitals, pair_list, pair_counts):
    count = lax.axis_size("orb")
    table = routes(count)
    device = lax.axis_index("orb")
    chip = (device % GROUP) // 2
    core = device % 2

    def send(value, name):
        return lax.ppermute(value, "orb", table[name])

    def placed(name, alternatives=1):
        held = jnp.array(HELD[name], jnp.int32)[chip]
        taker = jnp.array(TAKER[name], jnp.int32)[chip]
        offset = held - 2 * chip - core
        if name in ("y1", "y2"):
            return jnp.stack([jnp.where(core == taker, offset, NOWHERE), 0])
        choice = (core != taker).astype(jnp.int32)
        if name in ("x3", "y3"):
            choice = choice + 2 * jnp.array((1, 0, 0, 1), jnp.int32)[chip]
        return jnp.stack([offset, choice])

    listed = jnp.concatenate([pair_list, jnp.broadcast_to(pair_counts[:, None], (1, 2))], 0)
    behind = [
        lax.ppermute(listed, "orb", [(d, (d + distance) % count) for d in range(count)])
        for distance in range(1, REACH + 1)
    ]
    constants = [jnp.asarray(t) for t in tables(orbitals.shape[1])]

    partner = send(orbitals, "core")
    x1 = send(orbitals, "x1")
    y1 = send(orbitals, "y1")
    z1 = send(orbitals, "z1")
    lists = jnp.stack([listed] + behind)
    places = jnp.stack([1 - 2 * core, 0])[None]
    totals = visit_blocks(places, lists, orbitals, [[partner]], None, constants, True)

    held, x1, y1, z1 = lax.optimization_barrier((orbitals, x1, y1, z1))
    x2 = send(held, "x2")
    y2 = send(z1, "y2")
    z2 = send(x1, "z2")
    x1s = send(x1, "x1s")
    places = jnp.stack([placed("x1"), placed("y1")])
    totals = visit_blocks(places, lists, orbitals, [[x1, x1s], [y1]], totals, constants, False)

    x1, y1, x2, y2, z2 = lax.optimization_barrier((x1, y1, x2, y2, z2))
    x3a = send(y1, "x3a")
    x3b = send(y2, "x3b")
    y3a = send(x1, "y3a")
    y3b = send(z2, "y3b")
    x2s = send(x2, "x2s")
    places = jnp.stack([placed("x2"), placed("y2")])
    totals = visit_blocks(places, lists, orbitals, [[x2, x2s], [y2]], totals, constants, False)

    x3 = [x3a, send(x3a, "x3as"), x3b, send(x3b, "x3bs")]
    y3 = [y3a, send(y3a, "y3as"), y3b, send(y3b, "y3bs")]
    places = jnp.stack([placed("x3"), placed("y3")])
    return visit_blocks(places, lists, orbitals, [x3, y3], totals, constants, False)


def solution(mesh):
    return jax.shard_map(
        shards,
        mesh=mesh,
        in_specs=(P("orb", None, None), P("orb", None), P("orb")),
        out_specs=P("orb", None, None),
        check_vma=False,
    )
```

```python
import functools
import math

import jax
import jax.numpy as jnp
import numpy as np
from jax import lax
from jax.experimental import pallas as pl
from jax.experimental.pallas import tpu as pltpu
from jax.sharding import PartitionSpec as P

REACH = 3
LANES = 128
GROUP = 8
NOWHERE = 99
SETTLED = 16

screening = 0.5


def routes(count):
    groups = count // GROUP

    def device(group, chip, core):
        return (group % groups) * GROUP + 2 * chip + core

    names = ("x1", "x2", "x3a", "x3b", "y1", "y2", "y3a", "y3b", "z1", "z2")
    table = {name: [] for name in names}
    for g in range(groups):
        for c in range(4):
            first = 1 if c in (0, 2) else 0
            table["x1"].append((device(g, c, first), device(g, c ^ 1, first)))
            table["x2"].append((device(g, c, 1 - first), device(g, c ^ 1, 1 - first)))
            near = 1 if c in (0, 1) else 0
            table["y1"].append((device(g, c, near), device(g, c ^ 2, 1 - near)))
            edge = 1 if c in (2, 3) else 0
            step = 1 if c in (2, 3) else -1
            table["z1"].append((device(g, c, edge), device(g + step, c, edge)))
            table["y2"].append((device(g, c, edge), device(g, c ^ 2, 1 - edge)))
        table["z2"] += [(device(g, 2, 0), device(g + 1, 2, 0)), (device(g, 1, 1), device(g - 1, 1, 1))]
        table["x3a"] += [(device(g, 0, 1), device(g, 1, 1)), (device(g, 3, 0), device(g, 2, 0))]
        table["x3b"] += [(device(g, 1, 0), device(g, 0, 0)), (device(g, 2, 1), device(g, 3, 1))]
        table["y3a"] += [(device(g, 0, 0), device(g, 2, 0)), (device(g, 3, 1), device(g, 1, 1))]
        table["y3b"] += [(device(g, 2, 0), device(g, 0, 0)), (device(g, 1, 1), device(g, 3, 1))]
    table["core"] = [(d, d ^ 1) for d in range(count)]
    for name in ("x1", "x2", "x3a", "x3b", "y3a", "y3b"):
        table[name + "s"] = [(target, target ^ 1) for _, target in table[name]]
    return table


HELD = {
    "x1": (2, 1, 6, 5),
    "x2": (3, 0, 7, 4),
    "x3": (-1, 4, 3, 8),
    "y1": (4, 6, 1, 3),
    "y2": (-3, -1, 8, 10),
    "y3": (-2, 5, 2, 9),
}
TAKER = {
    "x1": (0, 1, 0, 1),
    "x2": (1, 0, 1, 0),
    "x3": (0, 1, 0, 1),
    "y1": (1, 1, 0, 0),
    "y2": (0, 0, 1, 1),
    "y3": (0, 1, 0, 1),
}


def places(names):
    table = np.zeros((GROUP, 2 * len(names)), np.int32)
    for position in range(GROUP):
        chip, core = divmod(position, 2)
        for at, name in enumerate(names):
            if name == "core":
                offset, choice = 1 - 2 * core, 0
            else:
                offset, choice = HELD[name][chip] - position, int(core != TAKER[name][chip])
            if name in ("y1", "y2"):
                offset, choice = (NOWHERE if choice else offset), 0
            if name in ("x3", "y3") and chip in (0, 3):
                choice += 2
            table[position, 2 * at : 2 * at + 2] = offset, choice
    return table


def tables(points):
    modes = np.arange(points) + 1.0
    sines = np.sin(math.pi * np.outer(modes, modes) / (points + 1)) * math.sqrt(2.0 / (points + 1))
    high = sines.astype(jnp.bfloat16)
    low = (sines - high.astype(np.float64)).astype(jnp.bfloat16)
    high, low = high.astype(np.float32), low.astype(np.float32)
    none = np.zeros_like(high)

    def straight(t):
        return np.block([[t, none], [none, t]])

    def crossed(t):
        return np.block([[none, t], [t, none]])

    def spread(form):
        return np.block([[form(high), form(low)], [form(high), form(low)]])

    along_lines = np.stack([spread(straight), spread(crossed)]).astype(jnp.bfloat16)
    along_planes = np.concatenate([high, high, low, low], 1).astype(jnp.bfloat16)
    eigen = 4.0 * np.sin(math.pi * modes / (2.0 * (points + 1))) ** 2
    diagonal = 2.0 + eigen[:, None] + eigen[None, :] + screening
    ratios = [1.0 / diagonal]
    for _ in range(min(points // 2, SETTLED) - 1):
        ratios.append(1.0 / (diagonal - ratios[-1]))
    middle = 1.0 / (1.0 - ratios[-1] ** 2)
    ratios = np.stack(ratios)
    ratios = np.concatenate([ratios, ratios], 2).astype(np.float32)
    middle = np.concatenate([middle, middle], 1).astype(np.float32)
    return along_lines, along_planes, ratios, middle


def split(value):
    high = value.astype(jnp.bfloat16)
    return high, (value - high.astype(jnp.float32)).astype(jnp.bfloat16)


def dot(left, right):
    return jnp.dot(left, right, preferred_element_type=jnp.float32)


def sine_lines(value, weights):
    product = dot(jnp.concatenate(split(value), 1), weights)
    return product[:, :LANES] + product[:, LANES:]


def sine_planes(value, weights):
    high, low = split(value)
    return dot(weights, jnp.concatenate([high, low, high, low], 0))


def tile(index):
    if isinstance(index, int):
        return pl.ds(index * LANES, LANES)
    return pl.ds(pl.multiple_of(index * LANES, LANES), LANES)


def potential_tiles(load_left, load_right, give, lines_ref, planes_ref, ratios_ref, middle_ref, kept, points):
    couples = points // 4
    last = 2 * couples - 1
    steps = ratios_ref.shape[0] - 1
    first_half = lax.broadcasted_iota(jnp.int32, (points, LANES), 1) < points
    even, odd = [], []
    for i in range(couples):
        near = load_left(i).astype(jnp.float32) * load_right(i).astype(jnp.float32)
        far = load_left(last - i).astype(jnp.float32) * load_right(last - i).astype(jnp.float32)
        even.append(jnp.where(first_half, near, far))
        odd.append(jnp.where(first_half, far, near))
    even = sine_lines(jnp.concatenate(even, 0), lines_ref[0])
    odd = sine_lines(jnp.concatenate(odd, 0), lines_ref[1])
    swept = jnp.zeros((points, LANES), jnp.float32)
    for i in range(couples):
        rows = slice(i * points, (i + 1) * points)
        modes = sine_planes(jnp.concatenate([even[rows], odd[rows]], 1), planes_ref[...])
        swept = (modes[:, :LANES] + swept) * ratios_ref[min(2 * i, steps)]
        kept[2 * i] = swept
        swept = (modes[:, LANES:] + swept) * ratios_ref[min(2 * i + 1, steps)]
        if i < couples - 1:
            kept[2 * i + 1] = swept
    solved = (swept + ratios_ref[min(last, steps)] * pltpu.roll(swept, points, 1)) * middle_ref[...]
    even, odd = [], []
    for i in reversed(range(couples)):
        if i < couples - 1:
            solved = kept[2 * i + 1] + ratios_ref[min(2 * i + 1, steps)] * solved
        later = solved
        solved = kept[2 * i] + ratios_ref[min(2 * i, steps)] * later
        grid = sine_planes(jnp.concatenate([solved, later], 1), planes_ref[...])
        even.append(grid[:, :LANES])
        odd.append(grid[:, LANES:])
    even = sine_lines(jnp.concatenate(even, 0), lines_ref[0])
    odd = sine_lines(jnp.concatenate(odd, 0), lines_ref[1])
    for place, i in enumerate(reversed(range(couples))):
        rows = slice(place * points, (place + 1) * points)
        give(i, jnp.where(first_half, even[rows], odd[rows]))
        give(last - i, jnp.where(first_half, odd[rows], even[rows]))


def visit_kernel(choices, fresh, with_own, points, *refs):
    refs = list(refs)
    places_ref, lists_ref, own_ref = refs[:3]
    sources, at = [], 3
    for count in choices:
        sources.append(refs[at : at + count])
        at += count
    if not fresh:
        before_ref = refs[at]
        at += 1
    lines_hbm, planes_hbm, ratios_hbm, middle_hbm, totals = refs[at : at + 5]
    window, lines_ref, planes_ref, ratios_ref, middle_ref, kept, extra, items, sems = refs[at + 5 :]
    own_count = own_ref.shape[0]
    slots = lists_ref.shape[1] - 1
    blocks = len(choices)
    position = lax.rem(lax.axis_index("orb"), GROUP)

    def brought(slot, source):
        return pltpu.make_async_copy(source, window.at[pl.ds((slot + 1) * own_count, own_count)], sems.at[slot + 1])

    own_copy = pltpu.make_async_copy(own_ref, window.at[pl.ds(0, own_count)], sems.at[0])
    own_copy.start()
    for slot in range(blocks):
        for choice, source in enumerate(sources[slot]):
            if len(sources[slot]) == 1:
                brought(slot, source).start()
            else:
                @pl.when(places_ref[position, 2 * slot + 1] == choice)
                def _():
                    brought(slot, source).start()
    constants = [
        pltpu.make_async_copy(source, target, sems.at[blocks + 2 + at])
        for at, (source, target) in enumerate(
            ((lines_hbm, lines_ref), (planes_hbm, planes_ref), (ratios_hbm, ratios_ref), (middle_hbm, middle_ref))
        )
    ]
    for copy in constants:
        copy.start()
    if fresh:
        totals[...] = jnp.zeros_like(totals)
    else:
        before = pltpu.make_async_copy(before_ref, totals, sems.at[blocks + 1])
        before.start()

    def note(keep, filled, own, other):
        @pl.when(keep)
        def _():
            items[filled, 0] = own
            items[filled, 1] = other

        return filled + keep.astype(jnp.int32)

    filled = jnp.int32(0)
    if with_own:
        def add_own(row, filled):
            keep = (row < lists_ref[0, slots, 0]) & (lists_ref[0, row, 1] < own_count)
            return note(keep, filled, lists_ref[0, row, 0], lists_ref[0, row, 1])

        filled = lax.fori_loop(0, slots, add_own, filled)
    for slot in range(blocks):
        offset = places_ref[position, 2 * slot]
        start = (slot + 1) * own_count
        ahead = offset > 0
        which = jnp.where(ahead, 0, jnp.minimum(-offset, REACH))
        distance = jnp.abs(offset)

        def add_block(row, filled):
            keep = (row < lists_ref[which, slots, 0]) & (lists_ref[which, row, 1] // own_count == distance)
            lead = lists_ref[which, row, 0]
            follow = lists_ref[which, row, 1] - distance * own_count
            return note(keep, filled, jnp.where(ahead, lead, follow), start + jnp.where(ahead, follow, lead))

        filled = lax.fori_loop(0, slots, add_block, filled)

    own_copy.wait()
    for slot in range(blocks):
        brought(slot, sources[slot][0]).wait()
    for copy in constants:
        copy.wait()
    if not fresh:
        before.wait()

    def visit(item, carried):
        mine = items[item, 0]
        other = items[item, 1]

        def load_mine(index):
            return window[mine, :, tile(index)]

        def load_other(index):
            return window[other, :, tile(index)]

        def give(index, potential):
            totals[mine, :, tile(index)] -= potential * load_other(index).astype(jnp.float32)
            if with_own:
                extra[:, tile(index)] = potential

        potential_tiles(
            load_mine, load_other, give, lines_ref, planes_ref, ratios_ref, middle_ref, kept, points
        )
        if with_own:
            @pl.when((other < own_count) & (other != mine))
            def _():
                def give_back(index, carried):
                    totals[other, :, tile(index)] -= extra[:, tile(index)] * load_mine(index).astype(jnp.float32)
                    return carried

                lax.fori_loop(0, points // 2, give_back, 0)

        return carried

    lax.fori_loop(0, filled, visit, 0)


def visit_blocks(names, lists, own, sources, before, constants, with_own):
    own_count, points, area = own.shape
    choices = tuple(len(source) for source in sources)
    flat = [array for source in sources for array in source]
    blocks = len(choices)
    vmem = pl.BlockSpec(memory_space=pltpu.VMEM)
    smem = pl.BlockSpec(memory_space=pltpu.SMEM)
    hbm = pl.BlockSpec(memory_space=pltpu.HBM)
    fresh = before is None
    most = (lists.shape[1] - 1) * (blocks + 1)
    pairs = 5
    return pl.pallas_call(
        functools.partial(visit_kernel, choices, fresh, with_own, points),
        out_shape=jax.ShapeDtypeStruct(own.shape, jnp.float32),
        in_specs=[smem, smem, hbm] + [hbm] * len(flat) + ([] if fresh else [hbm]) + [hbm] * len(constants),
        out_specs=vmem,
        scratch_shapes=[
            pltpu.VMEM(((blocks + 1) * own_count, points, area), jnp.bfloat16),
            *[pltpu.VMEM(table.shape, table.dtype) for table in constants],
            pltpu.VMEM((points // 2, points, LANES), jnp.float32),
            pltpu.VMEM((points, area) if with_own else (8, LANES), jnp.float32),
            pltpu.SMEM((most, 2), jnp.int32),
            pltpu.SemaphoreType.DMA((blocks + 2 + len(constants),)),
        ],
        compiler_params=pltpu.CompilerParams(vmem_limit_bytes=60 * 2**20),
        cost_estimate=pl.CostEstimate(
            flops=pairs * 8 * points * points * points * points * 8, bytes_accessed=16 * 2**20, transcendentals=0
        ),
    )(jnp.asarray(places(names)), lists, own, *flat, *([] if fresh else [before]), *constants)


def shards(orbitals, pair_list, pair_counts):
    count = lax.axis_size("orb")
    table = routes(count)

    def send(value, name):
        return lax.ppermute(value, "orb", table[name])

    listed = jnp.concatenate([pair_list, jnp.broadcast_to(pair_counts[:, None], (1, 2))], 0)
    behind = [
        lax.ppermute(listed, "orb", [(d, (d + distance) % count) for d in range(count)])
        for distance in range(1, REACH + 1)
    ]
    constants = [jnp.asarray(t) for t in tables(orbitals.shape[1])]

    partner = send(orbitals, "core")
    x1 = send(orbitals, "x1")
    y1 = send(orbitals, "y1")
    z1 = send(orbitals, "z1")
    lists = jnp.stack([listed] + behind)
    totals = visit_blocks(("core",), lists, orbitals, [[partner]], None, constants, True)

    held, x1, y1, z1, totals = lax.optimization_barrier((orbitals, x1, y1, z1, totals))
    x2 = send(held, "x2")
    y2 = send(z1, "y2")
    z2 = send(x1, "z2")
    x1s = send(x1, "x1s")
    totals = visit_blocks(("x1", "y1"), lists, orbitals, [[x1, x1s], [y1]], totals, constants, False)

    x1, y1, x2, y2, z2, totals = lax.optimization_barrier((x1, y1, x2, y2, z2, totals))
    x3a = send(y1, "x3a")
    x3b = send(y2, "x3b")
    y3a = send(x1, "y3a")
    y3b = send(z2, "y3b")
    x2s = send(x2, "x2s")
    totals = visit_blocks(("x2", "y2"), lists, orbitals, [[x2, x2s], [y2]], totals, constants, False)

    x3a, x3b, y3a, y3b, totals = lax.optimization_barrier((x3a, x3b, y3a, y3b, totals))
    x3 = [x3a, send(x3a, "x3as"), x3b, send(x3b, "x3bs")]
    y3 = [y3a, send(y3a, "y3as"), y3b, send(y3b, "y3bs")]
    return visit_blocks(("x3", "y3"), lists, orbitals, [x3, y3], totals, constants, False)


def solution(mesh):
    return jax.shard_map(
        shards,
        mesh=mesh,
        in_specs=(P("orb", None, None), P("orb", None), P("orb")),
        out_specs=P("orb", None, None),
        check_vma=False,
    )
```

```python
import functools
import math

import jax
import jax.numpy as jnp
import numpy as np
from jax import lax
from jax.experimental import pallas as pl
from jax.experimental.pallas import tpu as pltpu
from jax.sharding import PartitionSpec as P

REACH = 3
LANES = 128
GROUP = 8
VMEM_BYTES = 63 * 2**20
SETTLED = 16

screening = 0.5


def routes(count):
    groups = count // GROUP

    def device(group, chip, core):
        return (group % groups) * GROUP + 2 * chip + core

    names = ("x1", "x2", "x3_near", "x3_far", "y_near", "y_far", "y3_near", "y3_far")
    table = {name: [] for name in names}
    for g in range(groups):
        for c in range(4):
            early = 1 if c in (0, 2) else 0
            table["x1"].append((device(g, c, early), device(g, c ^ 1, early)))
            table["x2"].append((device(g, c, 1 - early), device(g, c ^ 1, 1 - early)))
            near = 1 if c in (0, 1) else 0
            table["y_near"].append((device(g, c, near), device(g, c ^ 2, 1 - near)))
            step = 1 if c in (2, 3) else -1
            table["y_far"].append((device(g, c, 1 - near), device(g + step, c ^ 2, near)))
        table["x3_near"] += [(device(g, 0, 1), device(g, 1, 1)), (device(g, 3, 0), device(g, 2, 0))]
        table["x3_far"] += [(device(g, 1, 0), device(g, 0, 0)), (device(g, 2, 1), device(g, 3, 1))]
        table["y3_near"] += [(device(g, 0, 0), device(g, 2, 0)), (device(g, 3, 1), device(g, 1, 1))]
        table["y3_far"] += [(device(g, 2, 0), device(g + 1, 0, 0)), (device(g, 1, 1), device(g - 1, 3, 1))]
    table["core"] = [(d, d ^ 1) for d in range(count)]
    for name in ("x1", "x2", "x3_near", "x3_far", "y3_near", "y3_far"):
        table[name + "_shared"] = [(target, target ^ 1) for _, target in table[name]]
    return table


HELD = {"x1": (2, 1, 6, 5), "x2": (3, 0, 7, 4), "x3": (-1, 4, 3, 8), "y3": (-2, 5, 2, 9)}
TAKER = {"x1": (0, 1, 0, 1), "x2": (1, 0, 1, 0), "x3": (0, 1, 0, 1), "y3": (0, 1, 0, 1)}


def places(names):
    table = np.zeros((GROUP, 2 * len(names)), np.int32)
    for position in range(GROUP):
        chip, core = divmod(position, 2)
        for at, name in enumerate(names):
            if name == "core":
                offset, choice = 1 - 2 * core, 0
            elif name == "y":
                offset, choice = (REACH if core else -REACH), int((chip < 2) != (core == 1))
            else:
                offset, choice = HELD[name][chip] - position, int(core != TAKER[name][chip])
            if name in ("x3", "y3") and chip in (0, 3):
                choice += 2
            table[position, 2 * at : 2 * at + 2] = offset, choice
    return table


def tables(points):
    modes = np.arange(points) + 1.0
    sines = np.sin(math.pi * np.outer(modes, modes) / (points + 1)) * math.sqrt(2.0 / (points + 1))
    high = sines.astype(jnp.bfloat16)
    low = (sines - high.astype(np.float64)).astype(jnp.bfloat16)
    high, low = high.astype(np.float32), low.astype(np.float32)
    none = np.zeros_like(high)

    def straight(t):
        return np.block([[t, none], [none, t]])

    def crossed(t):
        return np.block([[none, t], [t, none]])

    def spread(form):
        return np.block([[form(high), form(low)], [form(high), form(low)]])

    along_lines = np.stack([spread(straight), spread(crossed)]).astype(jnp.bfloat16)
    along_planes = np.concatenate([high, high, low], 1).astype(jnp.bfloat16)
    eigen = 4.0 * np.sin(math.pi * modes / (2.0 * (points + 1))) ** 2
    diagonal = 2.0 + eigen[:, None] + eigen[None, :] + screening
    ratios = [1.0 / diagonal]
    for _ in range(min(points // 2, SETTLED) - 1):
        ratios.append(1.0 / (diagonal - ratios[-1]))
    middle = 1.0 / (1.0 - ratios[-1] ** 2)
    ratios = np.stack(ratios)
    ratios = np.concatenate([ratios, ratios], 2).astype(np.float32)
    middle = np.concatenate([middle, middle], 1).astype(np.float32)
    return along_lines, along_planes, ratios, middle


def split(value):
    high = value.astype(jnp.bfloat16)
    return high, (value - high.astype(jnp.float32)).astype(jnp.bfloat16)


def dot(left, right):
    return jnp.dot(left, right, preferred_element_type=jnp.float32)


def sine_lines(value, weights):
    product = dot(jnp.concatenate(split(value), 1), weights)
    return product[:, :LANES] + product[:, LANES:]


def sine_planes(value, weights):
    high, low = split(value)
    return dot(weights, jnp.concatenate([high, low, high], 0))


def tile(index):
    if isinstance(index, int):
        return pl.ds(index * LANES, LANES)
    return pl.ds(pl.multiple_of(index * LANES, LANES), LANES)


def potential_tiles(load_left, load_right, give, ready, lines_ref, planes_ref, ratios_ref, middle_ref, kept, points):
    couples = points // 4
    last = 2 * couples - 1
    steps = ratios_ref.shape[0] - 1
    first_half = lax.broadcasted_iota(jnp.int32, (points, LANES), 1) < points
    even, odd = [], []
    for i in range(couples):
        near = load_left(i).astype(jnp.float32) * load_right(i).astype(jnp.float32)
        far = load_left(last - i).astype(jnp.float32) * load_right(last - i).astype(jnp.float32)
        even.append(jnp.where(first_half, near, far))
        odd.append(jnp.where(first_half, far, near))
    even = sine_lines(jnp.concatenate(even, 0), lines_ref[0])
    odd = sine_lines(jnp.concatenate(odd, 0), lines_ref[1])
    swept = jnp.zeros((points, LANES), jnp.float32)
    for i in range(couples):
        rows = slice(i * points, (i + 1) * points)
        modes = sine_planes(jnp.concatenate([even[rows], odd[rows]], 1), planes_ref[...])
        swept = (modes[:, :LANES] + swept) * ratios_ref[min(2 * i, steps)]
        kept[2 * i] = swept
        swept = (modes[:, LANES:] + swept) * ratios_ref[min(2 * i + 1, steps)]
        if i < couples - 1:
            kept[2 * i + 1] = swept
    solved = (swept + ratios_ref[min(last, steps)] * pltpu.roll(swept, points, 1)) * middle_ref[...]
    ready()
    even, odd = [], []
    for i in reversed(range(couples)):
        if i < couples - 1:
            solved = kept[2 * i + 1] + ratios_ref[min(2 * i + 1, steps)] * solved
        later = solved
        solved = kept[2 * i] + ratios_ref[min(2 * i, steps)] * later
        grid = sine_planes(jnp.concatenate([solved, later], 1), planes_ref[...])
        even.append(grid[:, :LANES])
        odd.append(grid[:, LANES:])
    even = sine_lines(jnp.concatenate(even, 0), lines_ref[0])
    odd = sine_lines(jnp.concatenate(odd, 0), lines_ref[1])
    for place, i in enumerate(reversed(range(couples))):
        rows = slice(place * points, (place + 1) * points)
        give(i, jnp.where(first_half, even[rows], odd[rows]))
        give(last - i, jnp.where(first_half, odd[rows], even[rows]))


def visit_kernel(choices, spans, lead_lists, fresh, with_own, points, *refs):
    refs = list(refs)
    places_ref = refs[0]
    lists_refs = refs[1 : 1 + lead_lists]
    own_ref = refs[1 + lead_lists]
    sources, at = [], 2 + lead_lists
    for count in choices:
        sources.append(refs[at : at + count])
        at += count
    if not fresh:
        before_ref = refs[at]
        at += 1
    lines_hbm, planes_hbm, ratios_hbm, middle_hbm, totals = refs[at : at + 5]
    window, lines_ref, planes_ref, ratios_ref, middle_ref, kept, extra, items, starts, sems = refs[at + 5 :]
    own_count = own_ref.shape[0]
    slots = lists_refs[0].shape[0] - 1
    blocks = len(choices)
    position = lax.rem(lax.axis_index("orb"), GROUP)

    bases = [own_count + sum(end - start for start, end in spans[:slot]) for slot in range(blocks)]

    def brought(slot, source):
        first, end = spans[slot]
        return pltpu.make_async_copy(source, window.at[pl.ds(bases[slot], end - first)], sems.at[slot + 1])

    own_copy = pltpu.make_async_copy(own_ref, window.at[pl.ds(0, own_count)], sems.at[0])
    own_copy.start()
    constants = [
        pltpu.make_async_copy(source, target, sems.at[blocks + 2 + at])
        for at, (source, target) in enumerate(
            ((lines_hbm, lines_ref), (planes_hbm, planes_ref), (ratios_hbm, ratios_ref), (middle_hbm, middle_ref))
        )
    ]
    for copy in constants:
        copy.start()
    for slot in range(blocks):
        for choice, source in enumerate(sources[slot]):
            if len(sources[slot]) == 1:
                brought(slot, source).start()
            else:
                @pl.when(places_ref[position, 2 * slot + 1] == choice)
                def _():
                    brought(slot, source).start()
    if fresh:
        totals[...] = jnp.zeros_like(totals)
    else:
        before = pltpu.make_async_copy(before_ref, totals, sems.at[blocks + 1])
        before.start()

    def note(keep, filled, own, other):
        @pl.when(keep)
        def _():
            items[filled, 0] = own
            items[filled, 1] = other

        return filled + keep.astype(jnp.int32)

    filled = jnp.int32(0)
    if with_own:
        own_list = lists_refs[0]

        def add_own(row, filled):
            keep = (row < own_list[slots, 0]) & (own_list[row, 1] < own_count)
            return note(keep, filled, own_list[row, 0], own_list[row, 1])

        filled = lax.fori_loop(0, slots, add_own, filled)
    for slot in range(blocks):
        offset = places_ref[position, 2 * slot]
        first, end = spans[slot]
        starts[slot] = filled
        for which, list_ref in enumerate(lists_refs):
            distance = offset if which == 0 else which
            active = offset > 0 if which == 0 else offset == -which
            live = jnp.where(active, list_ref[slots, 0], 0)

            def add_block(row, filled):
                lead = list_ref[row, 0]
                follow = list_ref[row, 1] - distance * own_count
                there = follow if which == 0 else lead
                keep = (follow >= 0) & (follow < own_count) & (there >= first) & (there < end)
                mine, other = (lead, follow) if which == 0 else (follow, lead)
                return note(keep, filled, mine, bases[slot] - first + other)

            filled = lax.fori_loop(0, live, add_block, filled)

    own_copy.wait()
    for copy in constants:
        copy.wait()

    def visit(item, carried):
        mine = items[item, 0]
        other = items[item, 1]
        for slot in range(blocks):
            @pl.when(item == starts[slot])
            def _():
                brought(slot, sources[slot][0]).wait()

        def load_mine(index):
            return window[mine, :, tile(index)]

        def load_other(index):
            return window[other, :, tile(index)]

        def give(index, potential):
            totals[mine, :, tile(index)] -= potential * load_other(index).astype(jnp.float32)
            if with_own:
                extra[:, tile(index)] = potential

        def ready():
            if not fresh:
                @pl.when(item == 0)
                def _():
                    before.wait()

        potential_tiles(
            load_mine, load_other, give, ready, lines_ref, planes_ref, ratios_ref, middle_ref, kept, points
        )
        if with_own:
            @pl.when((other < own_count) & (other != mine))
            def _():
                def give_back(index, carried):
                    totals[other, :, tile(index)] -= extra[:, tile(index)] * load_mine(index).astype(jnp.float32)
                    return carried

                lax.fori_loop(0, points // 2, give_back, 0)

        return carried

    lax.fori_loop(0, filled, visit, 0)
    for slot in range(blocks):
        @pl.when(starts[slot] == filled)
        def _():
            brought(slot, sources[slot][0]).wait()
    if not fresh:
        @pl.when(filled == 0)
        def _():
            before.wait()


def visit_blocks(blocks, lists, own, before, constants, with_own=False):
    own_count, points, area = own.shape
    names = [name for name, _, _ in blocks]
    spans = tuple((first, first + arrays[0].shape[0]) for _, first, arrays in blocks)
    choices = tuple(len(arrays) for _, _, arrays in blocks)
    fresh = before is None
    held = own_count + sum(end - first for first, end in spans)
    most = (lists[0].shape[0] - 1) * (len(blocks) + 1)
    passed = [own, *(array for _, _, arrays in blocks for array in arrays), *([] if fresh else [before]), *constants]
    return pl.pallas_call(
        functools.partial(visit_kernel, choices, spans, len(lists), fresh, with_own, points),
        out_shape=jax.ShapeDtypeStruct(own.shape, jnp.float32),
        in_specs=[pl.BlockSpec(memory_space=pltpu.SMEM)] * (1 + len(lists))
        + [pl.BlockSpec(memory_space=pl.ANY)] * len(passed),
        out_specs=pl.BlockSpec(memory_space=pltpu.VMEM),
        scratch_shapes=[
            pltpu.VMEM((held, points, area), jnp.bfloat16),
            *[pltpu.VMEM(table.shape, table.dtype) for table in constants],
            pltpu.VMEM((points // 2, points, LANES), jnp.float32),
            pltpu.VMEM((points, area) if with_own else (8, LANES), jnp.float32),
            pltpu.SMEM((most, 2), jnp.int32),
            pltpu.SMEM((len(blocks),), jnp.int32),
            pltpu.SemaphoreType.DMA((len(blocks) + 2 + len(constants),)),
        ],
        compiler_params=pltpu.CompilerParams(vmem_limit_bytes=VMEM_BYTES),
        cost_estimate=pl.CostEstimate(flops=0, bytes_accessed=0, transcendentals=0),
    )(jnp.asarray(places(names)), *lists, *passed)


def shards(orbitals, pair_list, pair_counts):
    count = lax.axis_size("orb")
    table = routes(count)
    constants = [jnp.asarray(t) for t in tables(orbitals.shape[1])]

    def send(value, name):
        return lax.ppermute(value, "orb", table[name])

    def spread(name, near, far):
        arrays = [near, send(near, name + "_near_shared"), far, send(far, name + "_far_shared")]
        return name, 0, arrays

    listed = jnp.concatenate([pair_list, jnp.broadcast_to(pair_counts[:, None], (1, 2))], 0)
    partner = send(orbitals, "core")
    x1 = send(orbitals, "x1")
    y_near = send(orbitals, "y_near")
    beside = send(listed, "core")
    later, partner = lax.optimization_barrier((listed, partner))
    behind = [
        lax.ppermute(later, "orb", [(d, (d + distance) % count) for d in range(count)])
        for distance in range(1, REACH + 1)
    ]
    totals = visit_blocks([("core", 0, [partner])], [listed, beside], orbitals, None, constants, True)

    held, x1, y_near, totals, *behind = lax.optimization_barrier((orbitals, x1, y_near, totals, *behind))
    lists = [listed] + behind
    x2 = send(held, "x2")
    y_far = send(held, "y_far")
    x1_shared = send(x1, "x1_shared")
    totals = visit_blocks([("x1", 0, [x1, x1_shared])], lists, orbitals, totals, constants)

    x1, x2, y_near, y_far, totals = lax.optimization_barrier((x1, x2, y_near, y_far, totals))
    x3_near = send(y_near, "x3_near")
    x3_far = send(y_far, "x3_far")
    y3_near = send(x1, "y3_near")
    y3_far = send(x1, "y3_far")
    x2_shared = send(x2, "x2_shared")
    blocks = [("x2", 0, [x2, x2_shared]), ("y", 0, [y_near, y_far])]
    totals = visit_blocks(blocks, lists, orbitals, totals, constants)

    x3_near, x3_far, y3_near, y3_far, totals = lax.optimization_barrier((x3_near, x3_far, y3_near, y3_far, totals))
    blocks = [spread("y3", y3_near, y3_far), spread("x3", x3_near, x3_far)]
    return visit_blocks(blocks, lists, orbitals, totals, constants)


def solution(mesh):
    return jax.shard_map(
        shards,
        mesh=mesh,
        in_specs=(P("orb", None, None), P("orb", None), P("orb")),
        out_specs=P("orb", None, None),
        check_vma=False,
    )
```

```python
import functools
import math

import jax
import jax.numpy as jnp
import numpy as np
from jax import lax
from jax.experimental import pallas as pl
from jax.experimental.pallas import tpu as pltpu
from jax.sharding import PartitionSpec as P

REACH = 3
LANES = 128
GROUP = 8
VMEM_BYTES = 63 * 2**20
SETTLED = 16

screening = 0.5


def routes(count):
    groups = count // GROUP

    def device(group, chip, core):
        return (group % groups) * GROUP + 2 * chip + core

    table = {"lead": [], "pass": [], "rest": []}
    for g in range(groups):
        lead = (
            ((0, 1), (g, 1, 1)), ((1, 0), (g, 0, 0)), ((2, 1), (g, 3, 1)), ((3, 0), (g, 2, 0)),
            ((0, 0), (g - 1, 2, 1)), ((1, 1), (g, 3, 0)), ((2, 0), (g, 0, 1)), ((3, 1), (g + 1, 1, 0)),
        )
        handed = (
            ((0, 1), (g, 1, 1)), ((3, 0), (g, 2, 0)), ((1, 0), (g, 0, 0)), ((2, 1), (g, 3, 1)),
            ((0, 0), (g, 2, 1)), ((3, 1), (g, 1, 0)), ((2, 0), (g + 1, 0, 1)), ((1, 1), (g - 1, 3, 0)),
        )
        rest = (
            ((0, 0), (g, 1, 0)), ((1, 1), (g, 0, 1)), ((2, 0), (g, 3, 0)), ((3, 1), (g, 2, 1)),
            ((0, 1), (g, 2, 0)), ((1, 0), (g - 1, 3, 1)), ((2, 1), (g + 1, 0, 0)), ((3, 0), (g, 1, 1)),
        )
        for name, moves in (("lead", lead), ("pass", handed), ("rest", rest)):
            table[name] += [(device(g, *sender), device(*taker)) for sender, taker in moves]
    table["core"] = [(d, d ^ 1) for d in range(count)]
    for name in ("lead", "rest"):
        table[name + "_shared"] = [
            (d, d ^ 1) for d in range(count) if abs(HELD[name][d % GROUP] - (d ^ 1) % GROUP) <= REACH
        ]
    table["pass_shared"] = table["core"]
    return table


HELD = {
    "core": (1, 0, 3, 2, 5, 4, 7, 6),
    "lead": (2, 4, -1, 1, 6, 8, 3, 5),
    "pass": (-1, -2, 5, 4, 3, 2, 9, 8),
    "rest": (-3, 3, 0, 6, 1, 7, 4, 10),
}


def offsets(names):
    table = np.zeros((GROUP, len(names)), np.int32)
    for position in range(GROUP):
        for at, (name, shared) in enumerate(names):
            table[position, at] = HELD[name][position ^ int(shared)] - position
    return table


def tables(points):
    modes = np.arange(points) + 1.0
    sines = np.sin(math.pi * np.outer(modes, modes) / (points + 1)) * math.sqrt(2.0 / (points + 1))
    high = sines.astype(jnp.bfloat16)
    low = (sines - high.astype(np.float64)).astype(jnp.bfloat16)
    high, low = high.astype(np.float32), low.astype(np.float32)
    none = np.zeros_like(high)

    def straight(t):
        return np.block([[t, none], [none, t]])

    def crossed(t):
        return np.block([[none, t], [t, none]])

    def spread(form):
        return np.block([[form(high), form(low)], [form(high), form(low)]])

    along_lines = np.stack([spread(straight), spread(crossed)]).astype(jnp.bfloat16)
    along_planes = np.concatenate([high, high, low], 1).astype(jnp.bfloat16)
    eigen = 4.0 * np.sin(math.pi * modes / (2.0 * (points + 1))) ** 2
    diagonal = 2.0 + eigen[:, None] + eigen[None, :] + screening
    ratios = [1.0 / diagonal]
    for _ in range(min(points // 2, SETTLED) - 1):
        ratios.append(1.0 / (diagonal - ratios[-1]))
    middle = 1.0 / (1.0 - ratios[-1] ** 2)
    ratios = np.stack(ratios)
    ratios = np.concatenate([ratios, ratios], 2).astype(np.float32)
    middle = np.concatenate([middle, middle], 1).astype(np.float32)
    return along_lines, along_planes, ratios, middle


def split(value):
    high = value.astype(jnp.bfloat16)
    return high, (value - high.astype(jnp.float32)).astype(jnp.bfloat16)


def dot(left, right):
    return jnp.dot(left, right, preferred_element_type=jnp.float32)


def sine_lines(value, weights):
    product = dot(jnp.concatenate(split(value), 1), weights)
    return product[:, :LANES] + product[:, LANES:]


def sine_planes(value, weights):
    high, low = split(value)
    return dot(weights, jnp.concatenate([high, low, high], 0))


def tile(index):
    if isinstance(index, int):
        return pl.ds(index * LANES, LANES)
    return pl.ds(pl.multiple_of(index * LANES, LANES), LANES)


def potential_tiles(load_left, load_right, give, ready, lines_ref, planes_ref, ratios_ref, middle_ref, kept, points):
    couples = points // 4
    last = 2 * couples - 1
    steps = ratios_ref.shape[0] - 1
    first_half = lax.broadcasted_iota(jnp.int32, (points, LANES), 1) < points
    even, odd = [], []
    for i in range(couples):
        near = load_left(i).astype(jnp.float32) * load_right(i).astype(jnp.float32)
        far = load_left(last - i).astype(jnp.float32) * load_right(last - i).astype(jnp.float32)
        even.append(jnp.where(first_half, near, far))
        odd.append(jnp.where(first_half, far, near))
    even = sine_lines(jnp.concatenate(even, 0), lines_ref[0])
    odd = sine_lines(jnp.concatenate(odd, 0), lines_ref[1])
    swept = jnp.zeros((points, LANES), jnp.float32)
    for i in range(couples):
        rows = slice(i * points, (i + 1) * points)
        modes = sine_planes(jnp.concatenate([even[rows], odd[rows]], 1), planes_ref[...])
        swept = (modes[:, :LANES] + swept) * ratios_ref[min(2 * i, steps)]
        kept[2 * i] = swept
        swept = (modes[:, LANES:] + swept) * ratios_ref[min(2 * i + 1, steps)]
        if i < couples - 1:
            kept[2 * i + 1] = swept
    solved = (swept + ratios_ref[min(last, steps)] * pltpu.roll(swept, points, 1)) * middle_ref[...]
    ready()
    even, odd = [], []
    for i in reversed(range(couples)):
        if i < couples - 1:
            solved = kept[2 * i + 1] + ratios_ref[min(2 * i + 1, steps)] * solved
        later = solved
        solved = kept[2 * i] + ratios_ref[min(2 * i, steps)] * later
        grid = sine_planes(jnp.concatenate([solved, later], 1), planes_ref[...])
        even.append(grid[:, :LANES])
        odd.append(grid[:, LANES:])
    even = sine_lines(jnp.concatenate(even, 0), lines_ref[0])
    odd = sine_lines(jnp.concatenate(odd, 0), lines_ref[1])
    for place, i in enumerate(reversed(range(couples))):
        rows = slice(place * points, (place + 1) * points)
        give(i, jnp.where(first_half, even[rows], odd[rows]))
        give(last - i, jnp.where(first_half, odd[rows], even[rows]))


def visit_kernel(blocks, lead_lists, fresh, with_own, points, *refs):
    refs = list(refs)
    offsets_ref = refs[0]
    lists_refs = refs[1 : 1 + lead_lists]
    own_ref = refs[1 + lead_lists]
    sources = refs[2 + lead_lists : 2 + lead_lists + blocks]
    at = 2 + lead_lists + blocks
    if not fresh:
        before_ref = refs[at]
        at += 1
    lines_hbm, planes_hbm, ratios_hbm, middle_hbm, totals = refs[at : at + 5]
    window, lines_ref, planes_ref, ratios_ref, middle_ref, kept, extra, items, starts, sems = refs[at + 5 :]
    own_count = own_ref.shape[0]
    slots = lists_refs[0].shape[0] - 1
    position = lax.rem(lax.axis_index("orb"), GROUP)

    def brought(slot):
        place = window.at[pl.ds((slot + 1) * own_count, own_count)]
        return pltpu.make_async_copy(sources[slot], place, sems.at[slot + 1])

    own_copy = pltpu.make_async_copy(own_ref, window.at[pl.ds(0, own_count)], sems.at[0])
    own_copy.start()
    constants = [
        pltpu.make_async_copy(source, target, sems.at[blocks + 2 + at])
        for at, (source, target) in enumerate(
            ((lines_hbm, lines_ref), (planes_hbm, planes_ref), (ratios_hbm, ratios_ref), (middle_hbm, middle_ref))
        )
    ]
    for copy in constants:
        copy.start()
    for slot in range(blocks):
        brought(slot).start()
    if fresh:
        totals[...] = jnp.zeros_like(totals)
    else:
        before = pltpu.make_async_copy(before_ref, totals, sems.at[blocks + 1])
        before.start()

    def note(keep, filled, own, other):
        @pl.when(keep)
        def _():
            items[filled, 0] = own
            items[filled, 1] = other

        return filled + keep.astype(jnp.int32)

    filled = jnp.int32(0)
    if with_own:
        own_list = lists_refs[0]

        def add_own(row, filled):
            keep = (row < own_list[slots, 0]) & (own_list[row, 1] < own_count)
            return note(keep, filled, own_list[row, 0], own_list[row, 1])

        filled = lax.fori_loop(0, slots, add_own, filled)
    for slot in range(blocks):
        offset = offsets_ref[position, slot]
        starts[slot] = filled
        for which, list_ref in enumerate(lists_refs):
            distance = offset if which == 0 else which
            active = offset > 0 if which == 0 else offset == -which
            live = jnp.where(active, list_ref[slots, 0], 0)

            def add_block(row, filled):
                lead = list_ref[row, 0]
                follow = list_ref[row, 1] - distance * own_count
                keep = (follow >= 0) & (follow < own_count)
                mine, other = (lead, follow) if which == 0 else (follow, lead)
                return note(keep, filled, mine, (slot + 1) * own_count + other)

            filled = lax.fori_loop(0, live, add_block, filled)

    own_copy.wait()
    for copy in constants:
        copy.wait()

    def visit(item, carried):
        mine = items[item, 0]
        other = items[item, 1]
        for slot in range(blocks):
            @pl.when(item == starts[slot])
            def _():
                brought(slot).wait()

        def load_mine(index):
            return window[mine, :, tile(index)]

        def load_other(index):
            return window[other, :, tile(index)]

        def give(index, potential):
            totals[mine, :, tile(index)] -= potential * load_other(index).astype(jnp.float32)
            if with_own:
                extra[:, tile(index)] = potential

        def ready():
            if not fresh:
                @pl.when(item == 0)
                def _():
                    before.wait()

        potential_tiles(
            load_mine, load_other, give, ready, lines_ref, planes_ref, ratios_ref, middle_ref, kept, points
        )
        if with_own:
            @pl.when((other < own_count) & (other != mine))
            def _():
                def give_back(index, carried):
                    totals[other, :, tile(index)] -= extra[:, tile(index)] * load_mine(index).astype(jnp.float32)
                    return carried

                lax.fori_loop(0, points // 2, give_back, 0)

        return carried

    lax.fori_loop(0, filled, visit, 0)
    for slot in range(blocks):
        @pl.when(starts[slot] == filled)
        def _():
            brought(slot).wait()
    if not fresh:
        @pl.when(filled == 0)
        def _():
            before.wait()


def visit_blocks(blocks, lists, own, before, constants, with_own=False):
    own_count, points, area = own.shape
    fresh = before is None
    most = (lists[0].shape[0] - 1) * (len(blocks) + 1)
    passed = [own, *(array for _, _, array in blocks), *([] if fresh else [before]), *constants]
    return pl.pallas_call(
        functools.partial(visit_kernel, len(blocks), len(lists), fresh, with_own, points),
        out_shape=jax.ShapeDtypeStruct(own.shape, jnp.float32),
        in_specs=[pl.BlockSpec(memory_space=pltpu.SMEM)] * (1 + len(lists))
        + [pl.BlockSpec(memory_space=pl.ANY)] * len(passed),
        out_specs=pl.BlockSpec(memory_space=pltpu.VMEM),
        scratch_shapes=[
            pltpu.VMEM(((len(blocks) + 1) * own_count, points, area), jnp.bfloat16),
            *[pltpu.VMEM(table.shape, table.dtype) for table in constants],
            pltpu.VMEM((points // 2, points, LANES), jnp.float32),
            pltpu.VMEM((points, area) if with_own else (8, LANES), jnp.float32),
            pltpu.SMEM((most, 2), jnp.int32),
            pltpu.SMEM((len(blocks),), jnp.int32),
            pltpu.SemaphoreType.DMA((len(blocks) + 2 + len(constants),)),
        ],
        compiler_params=pltpu.CompilerParams(vmem_limit_bytes=VMEM_BYTES),
        cost_estimate=pl.CostEstimate(flops=0, bytes_accessed=0, transcendentals=0),
    )(jnp.asarray(offsets([block[:2] for block in blocks])), *lists, *passed)


def shards(orbitals, pair_list, pair_counts):
    count = lax.axis_size("orb")
    table = routes(count)
    constants = [jnp.asarray(t) for t in tables(orbitals.shape[1])]

    def send(value, name):
        return lax.ppermute(value, "orb", table[name])

    listed = jnp.concatenate([pair_list, jnp.broadcast_to(pair_counts[:, None], (1, 2))], 0)
    partner = send(orbitals, "core")
    lead = send(orbitals, "lead")
    beside = send(listed, "core")
    later, partner = lax.optimization_barrier((listed, partner))
    behind = [
        lax.ppermute(later, "orb", [(d, (d + distance) % count) for d in range(count)])
        for distance in range(1, REACH + 1)
    ]
    totals = visit_blocks([("core", False, partner)], [listed, beside], orbitals, None, constants, True)

    lead, totals, *behind = lax.optimization_barrier((lead, totals, *behind))
    lists = [listed] + behind
    handed = send(lead, "pass")
    lead_shared = send(lead, "lead_shared")
    totals = visit_blocks([("lead", False, lead), ("lead", True, lead_shared)], lists, orbitals, totals, constants)

    held, handed, totals = lax.optimization_barrier((orbitals, handed, totals))
    rest = send(held, "rest")
    handed_shared = send(handed, "pass_shared")
    blocks = [("pass", False, handed), ("pass", True, handed_shared)]
    totals = visit_blocks(blocks, lists, orbitals, totals, constants)

    rest, totals = lax.optimization_barrier((rest, totals))
    rest_shared = send(rest, "rest_shared")
    return visit_blocks([("rest", False, rest), ("rest", True, rest_shared)], lists, orbitals, totals, constants)


def solution(mesh):
    return jax.shard_map(
        shards,
        mesh=mesh,
        in_specs=(P("orb", None, None), P("orb", None), P("orb")),
        out_specs=P("orb", None, None),
        check_vma=False,
    )
```

```python
import functools
import math

import jax
import jax.numpy as jnp
import numpy as np
from jax import lax
from jax.experimental import pallas as pl
from jax.experimental.pallas import tpu as pltpu
from jax.sharding import PartitionSpec as P

REACH = 3
LANES = 128
GROUP = 8
VMEM_BYTES = 32 * 2**20
SETTLED = 16

screening = 0.5


def routes(count):
    groups = count // GROUP

    def device(group, chip, core):
        return (group % groups) * GROUP + 2 * chip + core

    table = {"lead": [], "pass": [], "rest": []}
    for g in range(groups):
        lead = (
            ((0, 1), (g, 1, 1)), ((1, 0), (g, 0, 0)), ((2, 1), (g, 3, 1)), ((3, 0), (g, 2, 0)),
            ((0, 0), (g - 1, 2, 1)), ((1, 1), (g, 3, 0)), ((2, 0), (g, 0, 1)), ((3, 1), (g + 1, 1, 0)),
        )
        handed = (
            ((0, 1), (g, 1, 1)), ((3, 0), (g, 2, 0)), ((1, 0), (g, 0, 0)), ((2, 1), (g, 3, 1)),
            ((0, 0), (g, 2, 1)), ((3, 1), (g, 1, 0)), ((2, 0), (g + 1, 0, 1)), ((1, 1), (g - 1, 3, 0)),
        )
        rest = (
            ((0, 0), (g, 1, 0)), ((1, 1), (g, 0, 1)), ((2, 0), (g, 3, 0)), ((3, 1), (g, 2, 1)),
            ((0, 1), (g, 2, 0)), ((1, 0), (g - 1, 3, 1)), ((2, 1), (g + 1, 0, 0)), ((3, 0), (g, 1, 1)),
        )
        for name, moves in (("lead", lead), ("pass", handed), ("rest", rest)):
            table[name] += [(device(g, *sender), device(*taker)) for sender, taker in moves]
    table["core"] = [(d, d ^ 1) for d in range(count)]
    for name in ("lead", "rest"):
        table[name + "_shared"] = [
            (d, d ^ 1) for d in range(count) if abs(HELD[name][d % GROUP] - (d ^ 1) % GROUP) <= REACH
        ]
    table["pass_shared"] = table["core"]
    return table


HELD = {
    "core": (1, 0, 3, 2, 5, 4, 7, 6),
    "lead": (2, 4, -1, 1, 6, 8, 3, 5),
    "pass": (-1, -2, 5, 4, 3, 2, 9, 8),
    "rest": (-3, 3, 0, 6, 1, 7, 4, 10),
}


def offsets(names):
    table = np.zeros((GROUP, len(names)), np.int32)
    for position in range(GROUP):
        for at, (name, shared) in enumerate(names):
            table[position, at] = HELD[name][position ^ int(shared)] - position
    return table


def tables(points):
    modes = np.arange(points) + 1.0
    sines = np.sin(math.pi * np.outer(modes, modes) / (points + 1)) * math.sqrt(2.0 / (points + 1))
    high = sines.astype(jnp.bfloat16)
    low = (sines - high.astype(np.float64)).astype(jnp.bfloat16)
    high, low = high.astype(np.float32), low.astype(np.float32)
    none = np.zeros_like(high)

    def straight(t):
        return np.block([[t, none], [none, t]])

    def crossed(t):
        return np.block([[none, t], [t, none]])

    def spread(form):
        return np.block([[form(high), form(low)], [form(high), form(low)]])

    along_lines = np.stack([spread(straight), spread(crossed)]).astype(jnp.bfloat16)
    along_planes = np.concatenate([high, high, low], 1).astype(jnp.bfloat16)
    eigen = 4.0 * np.sin(math.pi * modes / (2.0 * (points + 1))) ** 2
    diagonal = 2.0 + eigen[:, None] + eigen[None, :] + screening
    ratios = [1.0 / diagonal]
    for _ in range(min(points // 2, SETTLED) - 1):
        ratios.append(1.0 / (diagonal - ratios[-1]))
    middle = 1.0 / (1.0 - ratios[-1] ** 2)
    ratios = np.stack(ratios)
    ratios = np.concatenate([ratios, ratios], 2).astype(np.float32)
    middle = np.concatenate([middle, middle], 1).astype(np.float32)
    return along_lines, along_planes, ratios, middle


def split(value):
    high = value.astype(jnp.bfloat16)
    return high, (value - high.astype(jnp.float32)).astype(jnp.bfloat16)


def dot(left, right):
    return jnp.dot(left, right, preferred_element_type=jnp.float32)


def sine_lines(value, weights):
    product = dot(jnp.concatenate(split(value), 1), weights)
    return product[:, :LANES] + product[:, LANES:]


def sine_planes(value, weights):
    high, low = split(value)
    return dot(weights, jnp.concatenate([high, low, high], 0))


def tile(index):
    if isinstance(index, int):
        return pl.ds(index * LANES, LANES)
    return pl.ds(pl.multiple_of(index * LANES, LANES), LANES)


def potential_tiles(load_left, load_right, give, ready, lines_ref, planes_ref, ratios_ref, middle_ref, kept, points):
    couples = points // 4
    last = 2 * couples - 1
    steps = ratios_ref.shape[0] - 1
    first_half = lax.broadcasted_iota(jnp.int32, (points, LANES), 1) < points
    even, odd = [], []
    for i in range(couples):
        near = load_left(i).astype(jnp.float32) * load_right(i).astype(jnp.float32)
        far = load_left(last - i).astype(jnp.float32) * load_right(last - i).astype(jnp.float32)
        even.append(jnp.where(first_half, near, far))
        odd.append(jnp.where(first_half, far, near))
    even = sine_lines(jnp.concatenate(even, 0), lines_ref[0])
    odd = sine_lines(jnp.concatenate(odd, 0), lines_ref[1])
    swept = jnp.zeros((points, LANES), jnp.float32)
    for i in range(couples):
        rows = slice(i * points, (i + 1) * points)
        modes = sine_planes(jnp.concatenate([even[rows], odd[rows]], 1), planes_ref[...])
        swept = (modes[:, :LANES] + swept) * ratios_ref[min(2 * i, steps)]
        kept[2 * i] = swept
        swept = (modes[:, LANES:] + swept) * ratios_ref[min(2 * i + 1, steps)]
        if i < couples - 1:
            kept[2 * i + 1] = swept
    solved = (swept + ratios_ref[min(last, steps)] * pltpu.roll(swept, points, 1)) * middle_ref[...]
    ready()
    even, odd = [], []
    for i in reversed(range(couples)):
        if i < couples - 1:
            solved = kept[2 * i + 1] + ratios_ref[min(2 * i + 1, steps)] * solved
        later = solved
        solved = kept[2 * i] + ratios_ref[min(2 * i, steps)] * later
        grid = sine_planes(jnp.concatenate([solved, later], 1), planes_ref[...])
        even.append(grid[:, :LANES])
        odd.append(grid[:, LANES:])
    even = sine_lines(jnp.concatenate(even, 0), lines_ref[0])
    odd = sine_lines(jnp.concatenate(odd, 0), lines_ref[1])
    for place, i in enumerate(reversed(range(couples))):
        rows = slice(place * points, (place + 1) * points)
        give(i, jnp.where(first_half, even[rows], odd[rows]))
        give(last - i, jnp.where(first_half, odd[rows], even[rows]))


def visit_kernel(blocks, lead_lists, fresh, with_own, points, *refs):
    refs = list(refs)
    offsets_ref = refs[0]
    lists_refs = refs[1 : 1 + lead_lists]
    own_ref = refs[1 + lead_lists]
    sources = refs[2 + lead_lists : 2 + lead_lists + blocks]
    at = 2 + lead_lists + blocks
    if not fresh:
        before_ref = refs[at]
        at += 1
    lines_hbm, planes_hbm, ratios_hbm, middle_hbm, totals = refs[at : at + 5]
    window, lines_ref, planes_ref, ratios_ref, middle_ref, kept, extra, items, starts, sems = refs[at + 5 :]
    own_count = own_ref.shape[0]
    slots = lists_refs[0].shape[0] - 1
    position = lax.rem(lax.axis_index("orb"), GROUP)

    def brought(slot):
        place = window.at[pl.ds((slot + 1) * own_count, own_count)]
        return pltpu.make_async_copy(sources[slot], place, sems.at[slot + 1])

    own_copy = pltpu.make_async_copy(own_ref, window.at[pl.ds(0, own_count)], sems.at[0])
    own_copy.start()
    constants = [
        pltpu.make_async_copy(source, target, sems.at[blocks + 2 + at])
        for at, (source, target) in enumerate(
            ((lines_hbm, lines_ref), (planes_hbm, planes_ref), (ratios_hbm, ratios_ref), (middle_hbm, middle_ref))
        )
    ]
    for copy in constants:
        copy.start()
    for slot in range(blocks):
        brought(slot).start()
    if fresh:
        totals[...] = jnp.zeros_like(totals)
    else:
        before = pltpu.make_async_copy(before_ref, totals, sems.at[blocks + 1])
        before.start()

    def note(keep, filled, own, other):
        @pl.when(keep)
        def _():
            items[filled, 0] = own
            items[filled, 1] = other

        return filled + keep.astype(jnp.int32)

    filled = jnp.int32(0)
    if with_own:
        own_list = lists_refs[0]

        def add_own(row, filled):
            keep = (row < own_list[slots, 0]) & (own_list[row, 1] < own_count)
            return note(keep, filled, own_list[row, 0], own_list[row, 1])

        filled = lax.fori_loop(0, slots, add_own, filled)
    for slot in range(blocks):
        offset = offsets_ref[position, slot]
        starts[slot] = filled
        for which, list_ref in enumerate(lists_refs):
            distance = offset if which == 0 else which
            active = offset > 0 if which == 0 else offset == -which
            live = jnp.where(active, list_ref[slots, 0], 0)

            def add_block(row, filled):
                lead = list_ref[row, 0]
                follow = list_ref[row, 1] - distance * own_count
                keep = (follow >= 0) & (follow < own_count)
                mine, other = (lead, follow) if which == 0 else (follow, lead)
                return note(keep, filled, mine, (slot + 1) * own_count + other)

            filled = lax.fori_loop(0, live, add_block, filled)

    own_copy.wait()
    for copy in constants:
        copy.wait()

    def visit(item, carried):
        mine = items[item, 0]
        other = items[item, 1]
        for slot in range(blocks):
            @pl.when(item == starts[slot])
            def _():
                brought(slot).wait()

        def load_mine(index):
            return window[mine, :, tile(index)]

        def load_other(index):
            return window[other, :, tile(index)]

        def give(index, potential):
            totals[mine, :, tile(index)] -= potential * load_other(index).astype(jnp.float32)
            if with_own:
                extra[:, tile(index)] = potential

        def ready():
            if not fresh:
                @pl.when(item == 0)
                def _():
                    before.wait()

        potential_tiles(
            load_mine, load_other, give, ready, lines_ref, planes_ref, ratios_ref, middle_ref, kept, points
        )
        if with_own:
            @pl.when((other < own_count) & (other != mine))
            def _():
                def give_back(index, carried):
                    totals[other, :, tile(index)] -= extra[:, tile(index)] * load_mine(index).astype(jnp.float32)
                    return carried

                lax.fori_loop(0, points // 2, give_back, 0)

        return carried

    lax.fori_loop(0, filled, visit, 0)
    for slot in range(blocks):
        @pl.when(starts[slot] == filled)
        def _():
            brought(slot).wait()
    if not fresh:
        @pl.when(filled == 0)
        def _():
            before.wait()


def visit_blocks(blocks, lists, own, before, constants, with_own=False):
    own_count, points, area = own.shape
    fresh = before is None
    most = (lists[0].shape[0] - 1) * (len(blocks) + 1)
    passed = [own, *(array for _, _, array in blocks), *([] if fresh else [before]), *constants]
    return pl.pallas_call(
        functools.partial(visit_kernel, len(blocks), len(lists), fresh, with_own, points),
        out_shape=jax.ShapeDtypeStruct(own.shape, jnp.float32),
        in_specs=[pl.BlockSpec(memory_space=pltpu.SMEM)] * (1 + len(lists))
        + [pl.BlockSpec(memory_space=pl.ANY)] * len(passed),
        out_specs=pl.BlockSpec(memory_space=pltpu.VMEM),
        scratch_shapes=[
            pltpu.VMEM(((len(blocks) + 1) * own_count, points, area), jnp.bfloat16),
            *[pltpu.VMEM(table.shape, table.dtype) for table in constants],
            pltpu.VMEM((points // 2, points, LANES), jnp.float32),
            pltpu.VMEM((points, area) if with_own else (8, LANES), jnp.float32),
            pltpu.SMEM((most, 2), jnp.int32),
            pltpu.SMEM((len(blocks),), jnp.int32),
            pltpu.SemaphoreType.DMA((len(blocks) + 2 + len(constants),)),
        ],
        compiler_params=pltpu.CompilerParams(vmem_limit_bytes=VMEM_BYTES),
        cost_estimate=pl.CostEstimate(flops=0, bytes_accessed=0, transcendentals=0),
    )(jnp.asarray(offsets([block[:2] for block in blocks])), *lists, *passed)


def shards(orbitals, pair_list, pair_counts):
    count = lax.axis_size("orb")
    table = routes(count)
    constants = [jnp.asarray(t) for t in tables(orbitals.shape[1])]

    def send(value, name):
        return lax.ppermute(value, "orb", table[name])

    listed = jnp.concatenate([pair_list, jnp.broadcast_to(pair_counts[:, None], (1, 2))], 0)
    partner = send(orbitals, "core")
    lead = send(orbitals, "lead")
    beside = send(listed, "core")
    later, partner = lax.optimization_barrier((listed, partner))
    behind = [
        lax.ppermute(later, "orb", [(d, (d + distance) % count) for d in range(count)])
        for distance in range(1, REACH + 1)
    ]
    totals = visit_blocks([("core", False, partner)], [listed, beside], orbitals, None, constants, True)

    lead, totals = lax.optimization_barrier((lead, totals))
    handed = send(lead, "pass")
    lead, *behind = lax.optimization_barrier((lead, *behind))
    lists = [listed] + behind
    lead_shared = send(lead, "lead_shared")
    totals = visit_blocks([("lead", False, lead), ("lead", True, lead_shared)], lists, orbitals, totals, constants)

    held, handed, totals = lax.optimization_barrier((orbitals, handed, totals))
    rest = send(held, "rest")
    handed_shared = send(handed, "pass_shared")
    blocks = [("pass", False, handed), ("pass", True, handed_shared)]
    totals = visit_blocks(blocks, lists, orbitals, totals, constants)

    rest, totals = lax.optimization_barrier((rest, totals))
    rest_shared = send(rest, "rest_shared")
    totals = visit_blocks([("rest", False, rest)], lists, orbitals, totals, constants)
    return visit_blocks([("rest", True, rest_shared)], lists, orbitals, totals, constants)


def solution(mesh):
    return jax.shard_map(
        shards,
        mesh=mesh,
        in_specs=(P("orb", None, None), P("orb", None), P("orb")),
        out_specs=P("orb", None, None),
        check_vma=False,
    )
```

```python
import functools
import math

import jax
import jax.numpy as jnp
import numpy as np
from jax import lax
from jax.experimental import pallas as pl
from jax.experimental.pallas import tpu as pltpu
from jax.sharding import PartitionSpec as P

REACH = 3
LANES = 128
GROUP = 8
VMEM_BYTES = 32 * 2**20
SETTLED = 16

screening = 0.5


def routes(count):
    groups = count // GROUP

    def device(group, chip, core):
        return (group % groups) * GROUP + 2 * chip + core

    table = {"lead": [], "pass": [], "rest": []}
    for g in range(groups):
        lead = (
            ((0, 1), (g, 1, 1)), ((1, 0), (g, 0, 0)), ((2, 1), (g, 3, 1)), ((3, 0), (g, 2, 0)),
            ((0, 0), (g - 1, 2, 1)), ((1, 1), (g, 3, 0)), ((2, 0), (g, 0, 1)), ((3, 1), (g + 1, 1, 0)),
        )
        handed = (
            ((0, 1), (g, 1, 1)), ((3, 0), (g, 2, 0)), ((1, 0), (g, 0, 0)), ((2, 1), (g, 3, 1)),
            ((0, 0), (g, 2, 1)), ((3, 1), (g, 1, 0)), ((2, 0), (g + 1, 0, 1)), ((1, 1), (g - 1, 3, 0)),
        )
        rest = (
            ((0, 0), (g, 1, 0)), ((1, 1), (g, 0, 1)), ((2, 0), (g, 3, 0)), ((3, 1), (g, 2, 1)),
            ((0, 1), (g, 2, 0)), ((1, 0), (g - 1, 3, 1)), ((2, 1), (g + 1, 0, 0)), ((3, 0), (g, 1, 1)),
        )
        for name, moves in (("lead", lead), ("pass", handed), ("rest", rest)):
            table[name] += [(device(g, *sender), device(*taker)) for sender, taker in moves]
    table["core"] = [(d, d ^ 1) for d in range(count)]
    for name in ("lead", "rest"):
        table[name + "_shared"] = [
            (d, d ^ 1) for d in range(count) if abs(HELD[name][d % GROUP] - (d ^ 1) % GROUP) <= REACH
        ]
    table["pass_shared"] = table["core"]
    return table


HELD = {
    "core": (1, 0, 3, 2, 5, 4, 7, 6),
    "lead": (2, 4, -1, 1, 6, 8, 3, 5),
    "pass": (-1, -2, 5, 4, 3, 2, 9, 8),
    "rest": (-3, 3, 0, 6, 1, 7, 4, 10),
}


def offsets(names):
    table = np.zeros((GROUP, len(names)), np.int32)
    for position in range(GROUP):
        for at, (name, shared) in enumerate(names):
            table[position, at] = HELD[name][position ^ int(shared)] - position
    return table


def tables(points):
    modes = np.arange(points) + 1.0
    sines = np.sin(math.pi * np.outer(modes, modes) / (points + 1)) * math.sqrt(2.0 / (points + 1))
    high = sines.astype(jnp.bfloat16)
    low = (sines - high.astype(np.float64)).astype(jnp.bfloat16)
    high, low = high.astype(np.float32), low.astype(np.float32)
    none = np.zeros_like(high)

    def straight(t):
        return np.block([[t, none], [none, t]])

    def crossed(t):
        return np.block([[none, t], [t, none]])

    def spread(form):
        return np.block([[form(high), form(low)], [form(high), form(low)]])

    along_lines = np.stack([spread(straight), spread(crossed)]).astype(jnp.bfloat16)
    along_planes = np.concatenate([high, high, low], 1).astype(jnp.bfloat16)
    eigen = 4.0 * np.sin(math.pi * modes / (2.0 * (points + 1))) ** 2
    diagonal = 2.0 + eigen[:, None] + eigen[None, :] + screening
    ratios = [1.0 / diagonal]
    for _ in range(min(points // 2, SETTLED) - 1):
        ratios.append(1.0 / (diagonal - ratios[-1]))
    middle = 1.0 / (1.0 - ratios[-1] ** 2)
    ratios = np.stack(ratios)
    ratios = np.concatenate([ratios, ratios], 2).astype(np.float32)
    middle = np.concatenate([middle, middle], 1).astype(np.float32)
    return along_lines, along_planes, ratios, middle


def split(value):
    high = value.astype(jnp.bfloat16)
    return high, (value - high.astype(jnp.float32)).astype(jnp.bfloat16)


def dot(left, right):
    return jnp.dot(left, right, preferred_element_type=jnp.float32)


def sine_lines(value, weights):
    product = dot(jnp.concatenate(split(value), 1), weights)
    return product[:, :LANES] + product[:, LANES:]


def sine_planes(value, weights):
    high, low = split(value)
    return dot(weights, jnp.concatenate([high, low, high], 0))


def tile(index):
    if isinstance(index, int):
        return pl.ds(index * LANES, LANES)
    return pl.ds(pl.multiple_of(index * LANES, LANES), LANES)


def potential_tiles(load_left, load_right, give, ready, lines_ref, planes_ref, ratios_ref, middle_ref, kept, points):
    couples = points // 4
    last = 2 * couples - 1
    steps = ratios_ref.shape[0] - 1
    first_half = lax.broadcasted_iota(jnp.int32, (points, LANES), 1) < points
    even, odd = [], []
    for i in range(couples):
        near = load_left(i).astype(jnp.float32) * load_right(i).astype(jnp.float32)
        far = load_left(last - i).astype(jnp.float32) * load_right(last - i).astype(jnp.float32)
        even.append(jnp.where(first_half, near, far))
        odd.append(jnp.where(first_half, far, near))
    even = sine_lines(jnp.concatenate(even, 0), lines_ref[0])
    odd = sine_lines(jnp.concatenate(odd, 0), lines_ref[1])
    swept = jnp.zeros((points, LANES), jnp.float32)
    for i in range(couples):
        rows = slice(i * points, (i + 1) * points)
        modes = sine_planes(jnp.concatenate([even[rows], odd[rows]], 1), planes_ref[...])
        swept = (modes[:, :LANES] + swept) * ratios_ref[min(2 * i, steps)]
        kept[2 * i] = swept
        swept = (modes[:, LANES:] + swept) * ratios_ref[min(2 * i + 1, steps)]
        if i < couples - 1:
            kept[2 * i + 1] = swept
    solved = (swept + ratios_ref[min(last, steps)] * pltpu.roll(swept, points, 1)) * middle_ref[...]
    ready()
    even, odd = [], []
    for i in reversed(range(couples)):
        if i < couples - 1:
            solved = kept[2 * i + 1] + ratios_ref[min(2 * i + 1, steps)] * solved
        later = solved
        solved = kept[2 * i] + ratios_ref[min(2 * i, steps)] * later
        grid = sine_planes(jnp.concatenate([solved, later], 1), planes_ref[...])
        even.append(grid[:, :LANES])
        odd.append(grid[:, LANES:])
    even = sine_lines(jnp.concatenate(even, 0), lines_ref[0])
    odd = sine_lines(jnp.concatenate(odd, 0), lines_ref[1])
    for place, i in enumerate(reversed(range(couples))):
        rows = slice(place * points, (place + 1) * points)
        give(i, jnp.where(first_half, even[rows], odd[rows]))
        give(last - i, jnp.where(first_half, odd[rows], even[rows]))


def visit_kernel(firsts, lead_lists, fresh, with_own, points, *refs):
    refs = list(refs)
    offsets_ref = refs[0]
    lists_refs = refs[1 : 1 + lead_lists]
    own_ref = refs[1 + lead_lists]
    blocks = len(firsts)
    sources = refs[2 + lead_lists : 2 + lead_lists + blocks]
    at = 2 + lead_lists + blocks
    if not fresh:
        before_ref = refs[at]
        at += 1
    lines_hbm, planes_hbm, ratios_hbm, middle_hbm, totals = refs[at : at + 5]
    window, lines_ref, planes_ref, ratios_ref, middle_ref, kept, extra, items, starts, sems = refs[at + 5 :]
    own_count = own_ref.shape[0]
    slots = lists_refs[0].shape[0] - 1
    position = lax.rem(lax.axis_index("orb"), GROUP)

    sizes = [source.shape[0] for source in sources]
    bases = [own_count + sum(sizes[:slot]) for slot in range(blocks)]

    def brought(slot):
        place = window.at[pl.ds(bases[slot], sizes[slot])]
        return pltpu.make_async_copy(sources[slot], place, sems.at[slot + 1])

    own_copy = pltpu.make_async_copy(own_ref, window.at[pl.ds(0, own_count)], sems.at[0])
    own_copy.start()
    constants = [
        pltpu.make_async_copy(source, target, sems.at[blocks + 2 + at])
        for at, (source, target) in enumerate(
            ((lines_hbm, lines_ref), (planes_hbm, planes_ref), (ratios_hbm, ratios_ref), (middle_hbm, middle_ref))
        )
    ]
    for copy in constants:
        copy.start()
    for slot in range(blocks):
        brought(slot).start()
    if fresh:
        totals[...] = jnp.zeros_like(totals)
    else:
        before = pltpu.make_async_copy(before_ref, totals, sems.at[blocks + 1])
        before.start()

    def note(keep, filled, own, other):
        @pl.when(keep)
        def _():
            items[filled, 0] = own
            items[filled, 1] = other

        return filled + keep.astype(jnp.int32)

    filled = jnp.int32(0)
    if with_own:
        own_list = lists_refs[0]

        def add_own(row, filled):
            keep = (row < own_list[slots, 0]) & (own_list[row, 1] < own_count)
            return note(keep, filled, own_list[row, 0], own_list[row, 1])

        filled = lax.fori_loop(0, slots, add_own, filled)
    for slot in range(blocks):
        offset = offsets_ref[position, slot]
        starts[slot] = filled
        for which, list_ref in enumerate(lists_refs):
            distance = offset if which == 0 else which
            active = offset > 0 if which == 0 else offset == -which
            live = jnp.where(active, list_ref[slots, 0], 0)

            def add_block(row, filled):
                lead = list_ref[row, 0]
                follow = list_ref[row, 1] - distance * own_count
                there = (follow if which == 0 else lead) - firsts[slot]
                keep = (follow >= 0) & (follow < own_count) & (there >= 0) & (there < sizes[slot])
                return note(keep, filled, lead if which == 0 else follow, bases[slot] + there)

            filled = lax.fori_loop(0, live, add_block, filled)

    own_copy.wait()
    for copy in constants:
        copy.wait()

    def visit(item, carried):
        mine = items[item, 0]
        other = items[item, 1]
        for slot in range(blocks):
            @pl.when(item == starts[slot])
            def _():
                brought(slot).wait()

        def load_mine(index):
            return window[mine, :, tile(index)]

        def load_other(index):
            return window[other, :, tile(index)]

        def give(index, potential):
            totals[mine, :, tile(index)] -= potential * load_other(index).astype(jnp.float32)
            if with_own:
                extra[:, tile(index)] = potential

        def ready():
            if not fresh:
                @pl.when(item == 0)
                def _():
                    before.wait()

        potential_tiles(
            load_mine, load_other, give, ready, lines_ref, planes_ref, ratios_ref, middle_ref, kept, points
        )
        if with_own:
            @pl.when((other < own_count) & (other != mine))
            def _():
                def give_back(index, carried):
                    totals[other, :, tile(index)] -= extra[:, tile(index)] * load_mine(index).astype(jnp.float32)
                    return carried

                lax.fori_loop(0, points // 2, give_back, 0)

        return carried

    lax.fori_loop(0, filled, visit, 0)
    for slot in range(blocks):
        @pl.when(starts[slot] == filled)
        def _():
            brought(slot).wait()
    if not fresh:
        @pl.when(filled == 0)
        def _():
            before.wait()


def visit_blocks(blocks, lists, own, before, constants, with_own=False):
    own_count, points, area = own.shape
    fresh = before is None
    most = (lists[0].shape[0] - 1) * (len(blocks) + 1)
    passed = [own, *(block[3] for block in blocks), *([] if fresh else [before]), *constants]
    return pl.pallas_call(
        functools.partial(visit_kernel, tuple(block[2] for block in blocks), len(lists), fresh, with_own, points),
        out_shape=jax.ShapeDtypeStruct(own.shape, jnp.float32),
        in_specs=[pl.BlockSpec(memory_space=pltpu.SMEM)] * (1 + len(lists))
        + [pl.BlockSpec(memory_space=pl.ANY)] * len(passed),
        out_specs=pl.BlockSpec(memory_space=pltpu.VMEM),
        scratch_shapes=[
            pltpu.VMEM((own_count + sum(block[3].shape[0] for block in blocks), points, area), jnp.bfloat16),
            *[pltpu.VMEM(table.shape, table.dtype) for table in constants],
            pltpu.VMEM((points // 2, points, LANES), jnp.float32),
            pltpu.VMEM((points, area) if with_own else (8, LANES), jnp.float32),
            pltpu.SMEM((most, 2), jnp.int32),
            pltpu.SMEM((len(blocks),), jnp.int32),
            pltpu.SemaphoreType.DMA((len(blocks) + 2 + len(constants),)),
        ],
        compiler_params=pltpu.CompilerParams(vmem_limit_bytes=VMEM_BYTES),
        cost_estimate=pl.CostEstimate(flops=0, bytes_accessed=0, transcendentals=0),
    )(jnp.asarray(offsets([block[:2] for block in blocks])), *lists, *passed)


def shards(orbitals, pair_list, pair_counts):
    count = lax.axis_size("orb")
    table = routes(count)
    constants = [jnp.asarray(t) for t in tables(orbitals.shape[1])]

    def send(value, name):
        return lax.ppermute(value, "orb", table[name])

    listed = jnp.concatenate([pair_list, jnp.broadcast_to(pair_counts[:, None], (1, 2))], 0)
    half = orbitals.shape[0] // 2
    partner = send(orbitals, "core")
    lead = send(orbitals, "lead")
    early = send(orbitals[:half], "rest")
    late = orbitals[half:]
    beside = send(listed, "core")
    later, partner = lax.optimization_barrier((listed, partner))
    behind = [
        lax.ppermute(later, "orb", [(d, (d + distance) % count) for d in range(count)])
        for distance in range(1, REACH + 1)
    ]
    totals = visit_blocks([("core", False, 0, partner)], [listed, beside], orbitals, None, constants, True)

    lead, early, late, totals, *behind = lax.optimization_barrier((lead, early, late, totals, *behind))
    lists = [listed] + behind
    handed = send(lead, "pass")
    lead_shared = send(lead, "lead_shared")
    early_shared = send(early, "rest_shared")
    blocks = [("lead", False, 0, lead), ("rest", False, 0, early)]
    blocks += [("lead", True, 0, lead_shared), ("rest", True, 0, early_shared)]
    totals = visit_blocks(blocks, lists, orbitals, totals, constants)

    late, handed, totals = lax.optimization_barrier((late, handed, totals))
    late = send(late, "rest")
    handed_shared = send(handed, "pass_shared")
    blocks = [("pass", False, 0, handed), ("pass", True, 0, handed_shared)]
    totals = visit_blocks(blocks, lists, orbitals, totals, constants)

    late, totals = lax.optimization_barrier((late, totals))
    late_shared = send(late, "rest_shared")
    totals = visit_blocks([("rest", False, half, late)], lists, orbitals, totals, constants)
    return visit_blocks([("rest", True, half, late_shared)], lists, orbitals, totals, constants)


def solution(mesh):
    return jax.shard_map(
        shards,
        mesh=mesh,
        in_specs=(P("orb", None, None), P("orb", None), P("orb")),
        out_specs=P("orb", None, None),
        check_vma=False,
    )
```

```python
import functools
import math

import jax
import jax.numpy as jnp
import numpy as np
from jax import lax
from jax.experimental import pallas as pl
from jax.experimental.pallas import tpu as pltpu
from jax.sharding import PartitionSpec as P

REACH = 3
LANES = 128
GROUP = 8
VMEM_BYTES = 32 * 2**20
GROUPS = 2
SETTLED = 16

screening = 0.5


def routes(count):
    groups = count // GROUP

    def device(group, chip, core):
        return (group % groups) * GROUP + 2 * chip + core

    table = {"lead": [], "pass": [], "rest": []}
    for g in range(groups):
        lead = (
            ((0, 1), (g, 1, 1)), ((1, 0), (g, 0, 0)), ((2, 1), (g, 3, 1)), ((3, 0), (g, 2, 0)),
            ((0, 0), (g - 1, 2, 1)), ((1, 1), (g, 3, 0)), ((2, 0), (g, 0, 1)), ((3, 1), (g + 1, 1, 0)),
        )
        handed = (
            ((0, 1), (g, 1, 1)), ((3, 0), (g, 2, 0)), ((1, 0), (g, 0, 0)), ((2, 1), (g, 3, 1)),
            ((0, 0), (g, 2, 1)), ((3, 1), (g, 1, 0)), ((2, 0), (g + 1, 0, 1)), ((1, 1), (g - 1, 3, 0)),
        )
        rest = (
            ((0, 0), (g, 1, 0)), ((1, 1), (g, 0, 1)), ((2, 0), (g, 3, 0)), ((3, 1), (g, 2, 1)),
            ((0, 1), (g, 2, 0)), ((1, 0), (g - 1, 3, 1)), ((2, 1), (g + 1, 0, 0)), ((3, 0), (g, 1, 1)),
        )
        for name, moves in (("lead", lead), ("pass", handed), ("rest", rest)):
            table[name] += [(device(g, *sender), device(*taker)) for sender, taker in moves]
    table["core"] = [(d, d ^ 1) for d in range(count)]
    for name in ("lead", "rest"):
        table[name + "_shared"] = [
            (d, d ^ 1) for d in range(count) if abs(HELD[name][d % GROUP] - (d ^ 1) % GROUP) <= REACH
        ]
    table["pass_shared"] = table["core"]
    return table


HELD = {
    "core": (1, 0, 3, 2, 5, 4, 7, 6),
    "lead": (2, 4, -1, 1, 6, 8, 3, 5),
    "pass": (-1, -2, 5, 4, 3, 2, 9, 8),
    "rest": (-3, 3, 0, 6, 1, 7, 4, 10),
}


def offsets(names):
    table = np.zeros((GROUP, len(names)), np.int32)
    for position in range(GROUP):
        for at, (name, shared) in enumerate(names):
            table[position, at] = HELD[name][position ^ int(shared)] - position
    return table


def tables(points):
    modes = np.arange(points) + 1.0
    sines = np.sin(math.pi * np.outer(modes, modes) / (points + 1)) * math.sqrt(2.0 / (points + 1))
    high = sines.astype(jnp.bfloat16)
    low = (sines - high.astype(np.float64)).astype(jnp.bfloat16)
    high, low = high.astype(np.float32), low.astype(np.float32)
    none = np.zeros_like(high)

    def straight(t):
        return np.block([[t, none], [none, t]])

    def crossed(t):
        return np.block([[none, t], [t, none]])

    def spread(form):
        return np.block([[form(high), form(low)], [form(high), form(low)]])

    along_lines = np.stack([spread(straight), spread(crossed)]).astype(jnp.bfloat16)
    along_planes = np.concatenate([high, high, low], 1).astype(jnp.bfloat16)
    eigen = 4.0 * np.sin(math.pi * modes / (2.0 * (points + 1))) ** 2
    diagonal = 2.0 + eigen[:, None] + eigen[None, :] + screening
    ratios = [1.0 / diagonal]
    for _ in range(min(points // 2, SETTLED) - 1):
        ratios.append(1.0 / (diagonal - ratios[-1]))
    middle = 1.0 / (1.0 - ratios[-1] ** 2)
    ratios = np.stack(ratios)
    ratios = np.concatenate([ratios, ratios], 2).astype(np.float32)
    middle = np.concatenate([middle, middle], 1).astype(np.float32)
    return along_lines, along_planes, ratios, middle


def split(value):
    high = value.astype(jnp.bfloat16)
    return high, (value - high.astype(jnp.float32)).astype(jnp.bfloat16)


def dot(left, right):
    return jnp.dot(left, right, preferred_element_type=jnp.float32)


def sine_lines(value, weights):
    product = dot(jnp.concatenate(split(value), 1), weights)
    return product[:, :LANES] + product[:, LANES:]


def sine_planes(value, weights):
    high, low = split(value)
    return dot(weights, jnp.concatenate([high, low, high], 0))


def tile(index):
    if isinstance(index, int):
        return pl.ds(index * LANES, LANES)
    return pl.ds(pl.multiple_of(index * LANES, LANES), LANES)


def forward_steps(load_left, load_right, put, tables, points, groups):
    lines_ref, planes_ref, ratios_ref, _ = tables
    couples = points // 4
    last = 2 * couples - 1
    size = couples // groups
    steps = ratios_ref.shape[0] - 1
    first_half = lax.broadcasted_iota(jnp.int32, (points, LANES), 1) < points
    state = {"swept": jnp.zeros((points, LANES), jnp.float32)}

    def lines(group):
        even, odd = [], []
        for i in range(group * size, (group + 1) * size):
            near = load_left(i).astype(jnp.float32) * load_right(i).astype(jnp.float32)
            far = load_left(last - i).astype(jnp.float32) * load_right(last - i).astype(jnp.float32)
            even.append(jnp.where(first_half, near, far))
            odd.append(jnp.where(first_half, far, near))
        state["even", group] = sine_lines(jnp.concatenate(even, 0), lines_ref[0])
        state["odd", group] = sine_lines(jnp.concatenate(odd, 0), lines_ref[1])

    def planes(group):
        even, odd = state.pop(("even", group)), state.pop(("odd", group))
        for place in range(size):
            rows = slice(place * points, (place + 1) * points)
            value = jnp.concatenate([even[rows], odd[rows]], 1)
            state["modes", group * size + place] = sine_planes(value, planes_ref[...])

    def sweep(group):
        for i in range(group * size, (group + 1) * size):
            modes = state.pop(("modes", i))
            swept = (modes[:, :LANES] + state["swept"]) * ratios_ref[min(2 * i, steps)]
            put(2 * i, swept)
            swept = (modes[:, LANES:] + swept) * ratios_ref[min(2 * i + 1, steps)]
            put(2 * i + 1, swept)
            state["swept"] = swept

    return lines, planes, sweep


def backward_steps(get, give, tables, points, groups):
    lines_ref, planes_ref, ratios_ref, middle_ref = tables
    couples = points // 4
    last = 2 * couples - 1
    size = couples // groups
    steps = ratios_ref.shape[0] - 1
    first_half = lax.broadcasted_iota(jnp.int32, (points, LANES), 1) < points
    state = {}

    def members(group):
        return range(couples - 1 - group * size, couples - 1 - (group + 1) * size, -1)

    def solve(group):
        if group == 0:
            swept = get(last)
            state["solved"] = (swept + ratios_ref[min(last, steps)] * pltpu.roll(swept, points, 1)) * middle_ref[...]
        for i in members(group):
            if i < couples - 1:
                state["solved"] = get(2 * i + 1) + ratios_ref[min(2 * i + 1, steps)] * state["solved"]
            later = state["solved"]
            state["solved"] = get(2 * i) + ratios_ref[min(2 * i, steps)] * later
            state["modes", i] = jnp.concatenate([state["solved"], later], 1)

    def planes(group):
        for i in members(group):
            state["grid", i] = sine_planes(state.pop(("modes", i)), planes_ref[...])

    def lines(group):
        grids = [state.pop(("grid", i)) for i in members(group)]
        state["even", group] = sine_lines(jnp.concatenate([grid[:, :LANES] for grid in grids], 0), lines_ref[0])
        state["odd", group] = sine_lines(jnp.concatenate([grid[:, LANES:] for grid in grids], 0), lines_ref[1])

    def hand(group):
        even, odd = state.pop(("even", group)), state.pop(("odd", group))
        for place, i in enumerate(members(group)):
            rows = slice(place * points, (place + 1) * points)
            give(i, jnp.where(first_half, even[rows], odd[rows]))
            give(last - i, jnp.where(first_half, odd[rows], even[rows]))

    return solve, planes, lines, hand


def run_forward(steps):
    lines, planes, sweep = steps
    lines(0)
    planes(0)
    sweep(0)


def run_backward(steps):
    for step in steps:
        step(0)


def run_both(forward, backward, groups):
    lines, planes, sweep = forward
    solve, planes_back, lines_back, hand = backward
    for stage in range(groups + 3):
        if stage < groups:
            lines(stage)
            solve(stage)
        if 0 <= stage - 1 < groups:
            planes_back(stage - 1)
            planes(stage - 1)
        if 0 <= stage - 2 < groups:
            lines_back(stage - 2)
            sweep(stage - 2)
        if 0 <= stage - 3 < groups:
            hand(stage - 3)


def visit_kernel(firsts, lead_lists, fresh, with_own, points, *refs):
    refs = list(refs)
    offsets_ref = refs[0]
    lists_refs = refs[1 : 1 + lead_lists]
    own_ref = refs[1 + lead_lists]
    blocks = len(firsts)
    sources = refs[2 + lead_lists : 2 + lead_lists + blocks]
    at = 2 + lead_lists + blocks
    if not fresh:
        before_ref = refs[at]
        at += 1
    lines_hbm, planes_hbm, ratios_hbm, middle_hbm, totals = refs[at : at + 5]
    window, lines_ref, planes_ref, ratios_ref, middle_ref, kept, extra, items, starts, sems = refs[at + 5 :]
    own_count = own_ref.shape[0]
    slots = lists_refs[0].shape[0] - 1
    position = lax.rem(lax.axis_index("orb"), GROUP)

    sizes = [source.shape[0] for source in sources]
    bases = [own_count + sum(sizes[:slot]) for slot in range(blocks)]

    def brought(slot):
        place = window.at[pl.ds(bases[slot], sizes[slot])]
        return pltpu.make_async_copy(sources[slot], place, sems.at[slot + 1])

    own_copy = pltpu.make_async_copy(own_ref, window.at[pl.ds(0, own_count)], sems.at[0])
    own_copy.start()
    constants = [
        pltpu.make_async_copy(source, target, sems.at[blocks + 2 + at])
        for at, (source, target) in enumerate(
            ((lines_hbm, lines_ref), (planes_hbm, planes_ref), (ratios_hbm, ratios_ref), (middle_hbm, middle_ref))
        )
    ]
    for copy in constants:
        copy.start()
    for slot in range(blocks):
        brought(slot).start()
    if fresh:
        totals[...] = jnp.zeros_like(totals)
    else:
        before = pltpu.make_async_copy(before_ref, totals, sems.at[blocks + 1])
        before.start()

    def note(keep, filled, own, other):
        @pl.when(keep)
        def _():
            items[filled, 0] = own
            items[filled, 1] = other

        return filled + keep.astype(jnp.int32)

    filled = jnp.int32(0)
    if with_own:
        own_list = lists_refs[0]

        def add_own(row, filled):
            keep = (row < own_list[slots, 0]) & (own_list[row, 1] < own_count)
            return note(keep, filled, own_list[row, 0], own_list[row, 1])

        filled = lax.fori_loop(0, slots, add_own, filled)
    for slot in range(blocks):
        offset = offsets_ref[position, slot]
        starts[slot] = filled
        for which, list_ref in enumerate(lists_refs):
            distance = offset if which == 0 else which
            active = offset > 0 if which == 0 else offset == -which
            live = jnp.where(active, list_ref[slots, 0], 0)

            def add_block(row, filled):
                lead = list_ref[row, 0]
                follow = list_ref[row, 1] - distance * own_count
                there = (follow if which == 0 else lead) - firsts[slot]
                keep = (follow >= 0) & (follow < own_count) & (there >= 0) & (there < sizes[slot])
                return note(keep, filled, lead if which == 0 else follow, bases[slot] + there)

            filled = lax.fori_loop(0, live, add_block, filled)

    own_copy.wait()
    for copy in constants:
        copy.wait()

    tables = (lines_ref, planes_ref, ratios_ref, middle_ref)

    def forward(item, groups):
        for slot in range(blocks):
            @pl.when(item == starts[slot])
            def _():
                brought(slot).wait()

        mine = items[item, 0]
        other = items[item, 1]
        side = lax.rem(item, 2)

        def put(index, swept):
            kept[side, index] = swept

        return forward_steps(
            lambda index: window[mine, :, tile(index)],
            lambda index: window[other, :, tile(index)],
            put, tables, points, groups,
        )

    def backward(item, groups):
        mine = items[item, 0]
        other = items[item, 1]
        side = lax.rem(item, 2)

        def give(index, potential):
            totals[mine, :, tile(index)] -= potential * window[other, :, tile(index)].astype(jnp.float32)
            if with_own:
                extra[:, tile(index)] = potential

        return backward_steps(lambda index: kept[side, index], give, tables, points, groups)

    def finish(item):
        if with_own:
            mine = items[item, 0]
            other = items[item, 1]

            @pl.when((other < own_count) & (other != mine))
            def _():
                def give_back(index, carried):
                    held = window[mine, :, tile(index)].astype(jnp.float32)
                    totals[other, :, tile(index)] -= extra[:, tile(index)] * held
                    return carried

                lax.fori_loop(0, points // 2, give_back, 0)

    @pl.when(filled > 0)
    def _():
        run_forward(forward(0, 1))

    if not fresh:
        before.wait()

    def visit(item, carried):
        run_both(forward(item, GROUPS), backward(item - 1, GROUPS), GROUPS)
        finish(item - 1)
        return carried

    lax.fori_loop(1, filled, visit, 0)

    @pl.when(filled > 0)
    def _():
        run_backward(backward(filled - 1, 1))
        finish(filled - 1)

    for slot in range(blocks):
        @pl.when(starts[slot] == filled)
        def _():
            brought(slot).wait()


def visit_blocks(blocks, lists, own, before, constants, with_own=False):
    own_count, points, area = own.shape
    fresh = before is None
    most = (lists[0].shape[0] - 1) * (len(blocks) + 1)
    passed = [own, *(block[3] for block in blocks), *([] if fresh else [before]), *constants]
    return pl.pallas_call(
        functools.partial(visit_kernel, tuple(block[2] for block in blocks), len(lists), fresh, with_own, points),
        out_shape=jax.ShapeDtypeStruct(own.shape, jnp.float32),
        in_specs=[pl.BlockSpec(memory_space=pltpu.SMEM)] * (1 + len(lists))
        + [pl.BlockSpec(memory_space=pl.ANY)] * len(passed),
        out_specs=pl.BlockSpec(memory_space=pltpu.VMEM),
        scratch_shapes=[
            pltpu.VMEM((own_count + sum(block[3].shape[0] for block in blocks), points, area), jnp.bfloat16),
            *[pltpu.VMEM(table.shape, table.dtype) for table in constants],
            pltpu.VMEM((2, points // 2, points, LANES), jnp.float32),
            pltpu.VMEM((points, area) if with_own else (8, LANES), jnp.float32),
            pltpu.SMEM((most, 2), jnp.int32),
            pltpu.SMEM((len(blocks),), jnp.int32),
            pltpu.SemaphoreType.DMA((len(blocks) + 2 + len(constants),)),
        ],
        compiler_params=pltpu.CompilerParams(vmem_limit_bytes=VMEM_BYTES),
        cost_estimate=pl.CostEstimate(flops=0, bytes_accessed=0, transcendentals=0),
    )(jnp.asarray(offsets([block[:2] for block in blocks])), *lists, *passed)


def shards(orbitals, pair_list, pair_counts):
    count = lax.axis_size("orb")
    table = routes(count)
    constants = [jnp.asarray(t) for t in tables(orbitals.shape[1])]

    def send(value, name):
        return lax.ppermute(value, "orb", table[name])

    listed = jnp.concatenate([pair_list, jnp.broadcast_to(pair_counts[:, None], (1, 2))], 0)
    half = orbitals.shape[0] // 2
    partner = send(orbitals, "core")
    lead = send(orbitals, "lead")
    early = send(orbitals[:half], "rest")
    late = orbitals[half:]
    beside = send(listed, "core")
    later, partner = lax.optimization_barrier((listed, partner))
    behind = [
        lax.ppermute(later, "orb", [(d, (d + distance) % count) for d in range(count)])
        for distance in range(1, REACH + 1)
    ]
    totals = visit_blocks([("core", False, 0, partner)], [listed, beside], orbitals, None, constants, True)

    lead, early, late, totals, *behind = lax.optimization_barrier((lead, early, late, totals, *behind))
    lists = [listed] + behind
    handed = send(lead, "pass")
    lead_shared = send(lead, "lead_shared")
    early_shared = send(early, "rest_shared")
    blocks = [("lead", False, 0, lead), ("rest", False, 0, early)]
    blocks += [("lead", True, 0, lead_shared), ("rest", True, 0, early_shared)]
    totals = visit_blocks(blocks, lists, orbitals, totals, constants)

    late, handed, totals = lax.optimization_barrier((late, handed, totals))
    late = send(late, "rest")
    handed_shared = send(handed, "pass_shared")
    blocks = [("pass", False, 0, handed), ("pass", True, 0, handed_shared)]
    totals = visit_blocks(blocks, lists, orbitals, totals, constants)

    late, totals = lax.optimization_barrier((late, totals))
    late_shared = send(late, "rest_shared")
    totals = visit_blocks([("rest", False, half, late)], lists, orbitals, totals, constants)
    return visit_blocks([("rest", True, half, late_shared)], lists, orbitals, totals, constants)


def solution(mesh):
    return jax.shard_map(
        shards,
        mesh=mesh,
        in_specs=(P("orb", None, None), P("orb", None), P("orb")),
        out_specs=P("orb", None, None),
        check_vma=False,
    )
```

```python
import functools
import math

import jax
import jax.numpy as jnp
import numpy as np
from jax import lax
from jax.experimental import pallas as pl
from jax.experimental.pallas import tpu as pltpu
from jax.sharding import PartitionSpec as P

REACH = 3
LANES = 128
GROUP = 8
VMEM_BYTES = 32 * 2**20
GROUPS = 2
SETTLED = 16

screening = 0.5


def routes(count):
    groups = count // GROUP

    def device(group, chip, core):
        return (group % groups) * GROUP + 2 * chip + core

    table = {"lead": [], "pass": [], "rest": []}
    for g in range(groups):
        lead = (
            ((0, 1), (g, 1, 1)), ((1, 0), (g, 0, 0)), ((2, 1), (g, 3, 1)), ((3, 0), (g, 2, 0)),
            ((0, 0), (g - 1, 2, 1)), ((1, 1), (g, 3, 0)), ((2, 0), (g, 0, 1)), ((3, 1), (g + 1, 1, 0)),
        )
        handed = (
            ((0, 1), (g, 1, 1)), ((3, 0), (g, 2, 0)), ((1, 0), (g, 0, 0)), ((2, 1), (g, 3, 1)),
            ((0, 0), (g, 2, 1)), ((3, 1), (g, 1, 0)), ((2, 0), (g + 1, 0, 1)), ((1, 1), (g - 1, 3, 0)),
        )
        rest = (
            ((0, 0), (g, 1, 0)), ((1, 1), (g, 0, 1)), ((2, 0), (g, 3, 0)), ((3, 1), (g, 2, 1)),
            ((0, 1), (g, 2, 0)), ((1, 0), (g - 1, 3, 1)), ((2, 1), (g + 1, 0, 0)), ((3, 0), (g, 1, 1)),
        )
        for name, moves in (("lead", lead), ("pass", handed), ("rest", rest)):
            table[name] += [(device(g, *sender), device(*taker)) for sender, taker in moves]
    table["core"] = [(d, d ^ 1) for d in range(count)]
    for name in ("lead", "rest"):
        table[name + "_shared"] = [
            (d, d ^ 1) for d in range(count) if abs(HELD[name][d % GROUP] - (d ^ 1) % GROUP) <= REACH
        ]
    table["pass_shared"] = table["core"]
    return table


HELD = {
    "core": (1, 0, 3, 2, 5, 4, 7, 6),
    "lead": (2, 4, -1, 1, 6, 8, 3, 5),
    "pass": (-1, -2, 5, 4, 3, 2, 9, 8),
    "rest": (-3, 3, 0, 6, 1, 7, 4, 10),
}


def offsets(names):
    table = np.zeros((GROUP, len(names)), np.int32)
    for position in range(GROUP):
        for at, (name, shared) in enumerate(names):
            table[position, at] = HELD[name][position ^ int(shared)] - position
    return table


def tables(points):
    modes = np.arange(points) + 1.0
    sines = np.sin(math.pi * np.outer(modes, modes) / (points + 1)) * math.sqrt(2.0 / (points + 1))
    high = sines.astype(jnp.bfloat16)
    low = (sines - high.astype(np.float64)).astype(jnp.bfloat16)
    high, low = high.astype(np.float32), low.astype(np.float32)
    none = np.zeros_like(high)

    def straight(t):
        return np.block([[t, none], [none, t]])

    def crossed(t):
        return np.block([[none, t], [t, none]])

    def spread(form):
        return np.block([[form(high), form(low)], [form(high), form(low)]])

    along_lines = np.stack([spread(straight), spread(crossed)]).astype(jnp.bfloat16)
    along_planes = np.concatenate([high, high, low], 1).astype(jnp.bfloat16)
    eigen = 4.0 * np.sin(math.pi * modes / (2.0 * (points + 1))) ** 2
    diagonal = 2.0 + eigen[:, None] + eigen[None, :] + screening
    ratios = [1.0 / diagonal]
    for _ in range(min(points // 2, SETTLED) - 1):
        ratios.append(1.0 / (diagonal - ratios[-1]))
    middle = 1.0 / (1.0 - ratios[-1] ** 2)
    ratios = np.stack(ratios)
    ratios = np.concatenate([ratios, ratios], 2).astype(np.float32)
    middle = np.concatenate([middle, middle], 1).astype(np.float32)
    return along_lines, along_planes, ratios, middle


def split(value):
    high = value.astype(jnp.bfloat16)
    return high, (value - high.astype(jnp.float32)).astype(jnp.bfloat16)


def dot(left, right):
    return jnp.dot(left, right, preferred_element_type=jnp.float32)


def sine_lines(value, weights):
    product = dot(jnp.concatenate(split(value), 1), weights)
    return product[:, :LANES] + product[:, LANES:]


def sine_planes(value, weights):
    high, low = split(value)
    return dot(weights, jnp.concatenate([high, low, high], 0))


def tile(index):
    if isinstance(index, int):
        return pl.ds(index * LANES, LANES)
    return pl.ds(pl.multiple_of(index * LANES, LANES), LANES)


def forward_steps(load_left, load_right, put, tables, points, groups):
    lines_ref, planes_ref, ratios_ref, _ = tables
    couples = points // 4
    last = 2 * couples - 1
    size = couples // groups
    steps = ratios_ref.shape[0] - 1
    first_half = lax.broadcasted_iota(jnp.int32, (points, LANES), 1) < points
    state = {"swept": jnp.zeros((points, LANES), jnp.float32)}

    def lines(group):
        even, odd = [], []
        for i in range(group * size, (group + 1) * size):
            near = load_left(i).astype(jnp.float32) * load_right(i).astype(jnp.float32)
            far = load_left(last - i).astype(jnp.float32) * load_right(last - i).astype(jnp.float32)
            even.append(jnp.where(first_half, near, far))
            odd.append(jnp.where(first_half, far, near))
        state["even", group] = sine_lines(jnp.concatenate(even, 0), lines_ref[0])
        state["odd", group] = sine_lines(jnp.concatenate(odd, 0), lines_ref[1])

    def planes(group):
        even, odd = state.pop(("even", group)), state.pop(("odd", group))
        for place in range(size):
            rows = slice(place * points, (place + 1) * points)
            value = jnp.concatenate([even[rows], odd[rows]], 1)
            state["modes", group * size + place] = sine_planes(value, planes_ref[...])

    def sweep(group):
        for i in range(group * size, (group + 1) * size):
            modes = state.pop(("modes", i))
            swept = (modes[:, :LANES] + state["swept"]) * ratios_ref[min(2 * i, steps)]
            put(2 * i, swept)
            swept = (modes[:, LANES:] + swept) * ratios_ref[min(2 * i + 1, steps)]
            put(2 * i + 1, swept)
            state["swept"] = swept

    return lines, planes, sweep


def backward_steps(get, give, tables, points, groups):
    lines_ref, planes_ref, ratios_ref, middle_ref = tables
    couples = points // 4
    last = 2 * couples - 1
    size = couples // groups
    steps = ratios_ref.shape[0] - 1
    first_half = lax.broadcasted_iota(jnp.int32, (points, LANES), 1) < points
    state = {}

    def members(group):
        return range(couples - 1 - group * size, couples - 1 - (group + 1) * size, -1)

    def solve(group):
        if group == 0:
            swept = get(last)
            state["solved"] = (swept + ratios_ref[min(last, steps)] * pltpu.roll(swept, points, 1)) * middle_ref[...]
        for i in members(group):
            if i < couples - 1:
                state["solved"] = get(2 * i + 1) + ratios_ref[min(2 * i + 1, steps)] * state["solved"]
            later = state["solved"]
            state["solved"] = get(2 * i) + ratios_ref[min(2 * i, steps)] * later
            state["modes", i] = jnp.concatenate([state["solved"], later], 1)

    def planes(group):
        for i in members(group):
            state["grid", i] = sine_planes(state.pop(("modes", i)), planes_ref[...])

    def lines(group):
        grids = [state.pop(("grid", i)) for i in members(group)]
        state["even", group] = sine_lines(jnp.concatenate([grid[:, :LANES] for grid in grids], 0), lines_ref[0])
        state["odd", group] = sine_lines(jnp.concatenate([grid[:, LANES:] for grid in grids], 0), lines_ref[1])

    def hand(group):
        even, odd = state.pop(("even", group)), state.pop(("odd", group))
        for place, i in enumerate(members(group)):
            rows = slice(place * points, (place + 1) * points)
            give(i, jnp.where(first_half, even[rows], odd[rows]))
            give(last - i, jnp.where(first_half, odd[rows], even[rows]))

    return solve, planes, lines, hand


def run_forward(steps):
    lines, planes, sweep = steps
    lines(0)
    planes(0)
    sweep(0)


def run_backward(steps):
    for step in steps:
        step(0)


def run_both(forward, backward, groups):
    lines, planes, sweep = forward
    solve, planes_back, lines_back, hand = backward
    for stage in range(groups + 3):
        if stage < groups:
            lines(stage)
            solve(stage)
        if 0 <= stage - 1 < groups:
            planes_back(stage - 1)
            planes(stage - 1)
        if 0 <= stage - 2 < groups:
            lines_back(stage - 2)
            sweep(stage - 2)
        if 0 <= stage - 3 < groups:
            hand(stage - 3)


def visit_kernel(firsts, lead_lists, fresh, with_own, streamed, points, *refs):
    refs = list(refs)
    offsets_ref = refs[0]
    lists_refs = refs[1 : 1 + lead_lists]
    own_ref = refs[1 + lead_lists]
    blocks = len(firsts)
    sources = refs[2 + lead_lists : 2 + lead_lists + blocks]
    at = 2 + lead_lists + blocks
    if not fresh:
        before_ref = refs[at]
        at += 1
    lines_hbm, planes_hbm, ratios_hbm, middle_hbm, totals = refs[at : at + 5]
    at += 5
    out_ref = totals
    if streamed:
        totals, touched, load_sems, out_sems = refs[-4:]
        refs = refs[:-4]
    window, lines_ref, planes_ref, ratios_ref, middle_ref, kept, extra, items, starts, sems = refs[at:]
    own_count = own_ref.shape[0]
    slots = lists_refs[0].shape[0] - 1
    position = lax.rem(lax.axis_index("orb"), GROUP)

    sizes = [source.shape[0] for source in sources]
    bases = [own_count + sum(sizes[:slot]) for slot in range(blocks)]

    def brought(slot):
        place = window.at[pl.ds(bases[slot], sizes[slot])]
        return pltpu.make_async_copy(sources[slot], place, sems.at[slot + 1])

    own_copy = pltpu.make_async_copy(own_ref, window.at[pl.ds(0, own_count)], sems.at[0])
    own_copy.start()
    constants = [
        pltpu.make_async_copy(source, target, sems.at[blocks + 2 + at])
        for at, (source, target) in enumerate(
            ((lines_hbm, lines_ref), (planes_hbm, planes_ref), (ratios_hbm, ratios_ref), (middle_hbm, middle_ref))
        )
    ]
    for copy in constants:
        copy.start()
    for slot in range(blocks):
        brought(slot).start()
    if fresh:
        totals[...] = jnp.zeros_like(totals)
    elif not streamed:
        before = pltpu.make_async_copy(before_ref, totals, sems.at[blocks + 1])
        before.start()
    else:
        loads = [pltpu.make_async_copy(before_ref.at[k], totals.at[k], load_sems.at[k]) for k in range(own_count)]
        leaves = [pltpu.make_async_copy(totals.at[k], out_ref.at[k], out_sems.at[k]) for k in range(own_count)]
        for k in range(own_count):
            loads[k].start()
            touched[k] = 0

    def note(keep, filled, own, other):
        @pl.when(keep)
        def _():
            items[filled, 0] = own
            items[filled, 1] = other
            if streamed:
                touched[own] = 1

        return filled + keep.astype(jnp.int32)

    filled = jnp.int32(0)
    if with_own:
        own_list = lists_refs[0]

        def add_own(row, filled):
            keep = (row < own_list[slots, 0]) & (own_list[row, 1] < own_count)
            return note(keep, filled, own_list[row, 0], own_list[row, 1])

        filled = lax.fori_loop(0, slots, add_own, filled)
    for slot in range(blocks):
        offset = offsets_ref[position, slot]
        starts[slot] = filled
        for which, list_ref in enumerate(lists_refs):
            distance = offset if which == 0 else which
            active = offset > 0 if which == 0 else offset == -which
            live = jnp.where(active, list_ref[slots, 0], 0)

            def add_block(row, filled):
                lead = list_ref[row, 0]
                follow = list_ref[row, 1] - distance * own_count
                there = (follow if which == 0 else lead) - firsts[slot]
                keep = (follow >= 0) & (follow < own_count) & (there >= 0) & (there < sizes[slot])
                return note(keep, filled, lead if which == 0 else follow, bases[slot] + there)

            filled = lax.fori_loop(0, live, add_block, filled)

    own_copy.wait()
    for copy in constants:
        copy.wait()

    tables = (lines_ref, planes_ref, ratios_ref, middle_ref)

    def forward(item, groups):
        for slot in range(blocks):
            @pl.when(item == starts[slot])
            def _():
                brought(slot).wait()

        mine = items[item, 0]
        other = items[item, 1]
        side = lax.rem(item, 2)

        def put(index, swept):
            kept[side, index] = swept

        return forward_steps(
            lambda index: window[mine, :, tile(index)],
            lambda index: window[other, :, tile(index)],
            put, tables, points, groups,
        )

    def backward(item, groups):
        mine = items[item, 0]
        other = items[item, 1]
        side = lax.rem(item, 2)

        def give(index, potential):
            totals[mine, :, tile(index)] -= potential * window[other, :, tile(index)].astype(jnp.float32)
            if with_own:
                extra[:, tile(index)] = potential

        return backward_steps(lambda index: kept[side, index], give, tables, points, groups)

    def finish(item):
        if with_own:
            mine = items[item, 0]
            other = items[item, 1]

            @pl.when((other < own_count) & (other != mine))
            def _():
                def give_back(index, carried):
                    held = window[mine, :, tile(index)].astype(jnp.float32)
                    totals[other, :, tile(index)] -= extra[:, tile(index)] * held
                    return carried

                lax.fori_loop(0, points // 2, give_back, 0)

    @pl.when(filled > 0)
    def _():
        run_forward(forward(0, 1))

    if streamed:
        for k in range(own_count):
            loads[k].wait()

            @pl.when(touched[k] == 0)
            def _():
                leaves[k].start()
    elif not fresh:
        before.wait()

    def visit(item, carried):
        run_both(forward(item, GROUPS), backward(item - 1, GROUPS), GROUPS)
        finish(item - 1)
        return carried

    lax.fori_loop(1, filled, visit, 0)

    @pl.when(filled > 0)
    def _():
        run_backward(backward(filled - 1, 1))
        finish(filled - 1)

    if streamed:
        for k in range(own_count):
            @pl.when(touched[k] != 0)
            def _():
                leaves[k].start()
    for slot in range(blocks):
        @pl.when(starts[slot] == filled)
        def _():
            brought(slot).wait()
    if streamed:
        for copy in leaves:
            copy.wait()


def visit_blocks(blocks, lists, own, before, constants, with_own=False, streamed=False):
    own_count, points, area = own.shape
    fresh = before is None
    most = (lists[0].shape[0] - 1) * (len(blocks) + 1)
    passed = [own, *(block[3] for block in blocks), *([] if fresh else [before]), *constants]
    return pl.pallas_call(
        functools.partial(visit_kernel, tuple(block[2] for block in blocks), len(lists), fresh, with_own, streamed, points),
        out_shape=jax.ShapeDtypeStruct(own.shape, jnp.float32),
        in_specs=[pl.BlockSpec(memory_space=pltpu.SMEM)] * (1 + len(lists))
        + [pl.BlockSpec(memory_space=pl.ANY)] * len(passed),
        out_specs=pl.BlockSpec(memory_space=pl.ANY if streamed else pltpu.VMEM),
        scratch_shapes=[
            pltpu.VMEM((own_count + sum(block[3].shape[0] for block in blocks), points, area), jnp.bfloat16),
            *[pltpu.VMEM(table.shape, table.dtype) for table in constants],
            pltpu.VMEM((2, points // 2, points, LANES), jnp.float32),
            pltpu.VMEM((points, area) if with_own else (8, LANES), jnp.float32),
            pltpu.SMEM((most, 2), jnp.int32),
            pltpu.SMEM((len(blocks),), jnp.int32),
            pltpu.SemaphoreType.DMA((len(blocks) + 2 + len(constants),)),
            *(
                [
                    pltpu.VMEM(own.shape, jnp.float32),
                    pltpu.SMEM((own_count,), jnp.int32),
                    pltpu.SemaphoreType.DMA((own_count,)),
                    pltpu.SemaphoreType.DMA((own_count,)),
                ]
                if streamed
                else []
            ),
        ],
        compiler_params=pltpu.CompilerParams(vmem_limit_bytes=VMEM_BYTES),
        cost_estimate=pl.CostEstimate(flops=0, bytes_accessed=0, transcendentals=0),
    )(jnp.asarray(offsets([block[:2] for block in blocks])), *lists, *passed)


def shards(orbitals, pair_list, pair_counts):
    count = lax.axis_size("orb")
    table = routes(count)
    constants = [jnp.asarray(t) for t in tables(orbitals.shape[1])]

    def send(value, name):
        return lax.ppermute(value, "orb", table[name])

    listed = jnp.concatenate([pair_list, jnp.broadcast_to(pair_counts[:, None], (1, 2))], 0)
    cut = max(orbitals.shape[0] // 4, 1)
    partner = send(orbitals, "core")
    lead = send(orbitals, "lead")
    early = send(orbitals[:cut], "rest")
    late = orbitals[cut:]
    beside = send(listed, "core")
    later, partner = lax.optimization_barrier((listed, partner))
    behind = [
        lax.ppermute(later, "orb", [(d, (d + distance) % count) for d in range(count)])
        for distance in range(1, REACH + 1)
    ]
    totals = visit_blocks([("core", False, 0, partner)], [listed, beside], orbitals, None, constants, True)

    lead, early, late, totals, *behind = lax.optimization_barrier((lead, early, late, totals, *behind))
    lists = [listed] + behind
    handed = send(lead, "pass")
    lead_shared = send(lead, "lead_shared")
    early_shared = send(early, "rest_shared")
    blocks = [("lead", False, 0, lead), ("rest", False, 0, early)]
    blocks += [("lead", True, 0, lead_shared), ("rest", True, 0, early_shared)]
    totals = visit_blocks(blocks, lists, orbitals, totals, constants)

    late, handed, totals = lax.optimization_barrier((late, handed, totals))
    late = send(late, "rest")
    handed_shared = send(handed, "pass_shared")
    blocks = [("pass", False, 0, handed), ("pass", True, 0, handed_shared)]
    totals = visit_blocks(blocks, lists, orbitals, totals, constants)

    late, totals = lax.optimization_barrier((late, totals))
    late_shared = send(late, "rest_shared")
    totals = visit_blocks([("rest", False, cut, late)], lists, orbitals, totals, constants)
    return visit_blocks([("rest", True, cut, late_shared)], lists, orbitals, totals, constants, streamed=True)


def solution(mesh):
    return jax.shard_map(
        shards,
        mesh=mesh,
        in_specs=(P("orb", None, None), P("orb", None), P("orb")),
        out_specs=P("orb", None, None),
        check_vma=False,
    )
```

```python
import functools
import math

import jax
import jax.numpy as jnp
import numpy as np
from jax import lax
from jax.experimental import pallas as pl
from jax.experimental.pallas import tpu as pltpu
from jax.sharding import PartitionSpec as P

REACH = 3
LANES = 128
GROUP = 8
VMEM_BYTES = 32 * 2**20
GROUPS = 2
SETTLED = 16

screening = 0.5


def routes(count):
    groups = count // GROUP

    def device(group, chip, core):
        return (group % groups) * GROUP + 2 * chip + core

    table = {"lead": [], "pass": [], "rest": []}
    for g in range(groups):
        lead = (
            ((0, 1), (g, 1, 1)), ((1, 0), (g, 0, 0)), ((2, 1), (g, 3, 1)), ((3, 0), (g, 2, 0)),
            ((0, 0), (g - 1, 2, 1)), ((1, 1), (g, 3, 0)), ((2, 0), (g, 0, 1)), ((3, 1), (g + 1, 1, 0)),
        )
        handed = (
            ((0, 1), (g, 1, 1)), ((3, 0), (g, 2, 0)), ((1, 0), (g, 0, 0)), ((2, 1), (g, 3, 1)),
            ((0, 0), (g, 2, 1)), ((3, 1), (g, 1, 0)), ((2, 0), (g + 1, 0, 1)), ((1, 1), (g - 1, 3, 0)),
        )
        rest = (
            ((0, 0), (g, 1, 0)), ((1, 1), (g, 0, 1)), ((2, 0), (g, 3, 0)), ((3, 1), (g, 2, 1)),
            ((0, 1), (g, 2, 0)), ((1, 0), (g - 1, 3, 1)), ((2, 1), (g + 1, 0, 0)), ((3, 0), (g, 1, 1)),
        )
        for name, moves in (("lead", lead), ("pass", handed), ("rest", rest)):
            table[name] += [(device(g, *sender), device(*taker)) for sender, taker in moves]
    table["core"] = [(d, d ^ 1) for d in range(count)]
    for name in ("lead", "rest"):
        table[name + "_shared"] = [
            (d, d ^ 1) for d in range(count) if abs(HELD[name][d % GROUP] - (d ^ 1) % GROUP) <= REACH
        ]
    table["pass_shared"] = table["core"]
    return table


HELD = {
    "core": (1, 0, 3, 2, 5, 4, 7, 6),
    "lead": (2, 4, -1, 1, 6, 8, 3, 5),
    "pass": (-1, -2, 5, 4, 3, 2, 9, 8),
    "rest": (-3, 3, 0, 6, 1, 7, 4, 10),
}


def offsets(names):
    table = np.zeros((GROUP, len(names)), np.int32)
    for position in range(GROUP):
        for at, (name, shared) in enumerate(names):
            table[position, at] = HELD[name][position ^ int(shared)] - position
    return table


def tables(points):
    modes = np.arange(points) + 1.0
    sines = np.sin(math.pi * np.outer(modes, modes) / (points + 1)) * math.sqrt(2.0 / (points + 1))
    high = sines.astype(jnp.bfloat16)
    low = (sines - high.astype(np.float64)).astype(jnp.bfloat16)
    high, low = high.astype(np.float32), low.astype(np.float32)
    none = np.zeros_like(high)

    def straight(t):
        return np.block([[t, none], [none, t]])

    def crossed(t):
        return np.block([[none, t], [t, none]])

    def spread(form):
        return np.block([[form(high), form(low)], [form(high), form(low)]])

    along_lines = np.stack([spread(straight), spread(crossed)]).astype(jnp.bfloat16)
    along_planes = np.concatenate([high, high, low], 1).astype(jnp.bfloat16)
    eigen = 4.0 * np.sin(math.pi * modes / (2.0 * (points + 1))) ** 2
    diagonal = 2.0 + eigen[:, None] + eigen[None, :] + screening
    ratios = [1.0 / diagonal]
    for _ in range(min(points // 2, SETTLED) - 1):
        ratios.append(1.0 / (diagonal - ratios[-1]))
    middle = 1.0 / (1.0 - ratios[-1] ** 2)
    ratios = np.stack(ratios)
    ratios = np.concatenate([ratios, ratios], 2).astype(np.float32)
    middle = np.concatenate([middle, middle], 1).astype(np.float32)
    return along_lines, along_planes, ratios, middle


def split(value):
    high = value.astype(jnp.bfloat16)
    return high, (value - high.astype(jnp.float32)).astype(jnp.bfloat16)


def dot(left, right):
    return jnp.dot(left, right, preferred_element_type=jnp.float32)


def sine_lines(value, weights):
    product = dot(jnp.concatenate(split(value), 1), weights)
    return product[:, :LANES] + product[:, LANES:]


def sine_planes(value, weights):
    high, low = split(value)
    return dot(weights, jnp.concatenate([high, low, high], 0))


def tile(index):
    if isinstance(index, int):
        return pl.ds(index * LANES, LANES)
    return pl.ds(pl.multiple_of(index * LANES, LANES), LANES)


def forward_steps(load_left, load_right, put, tables, points, groups):
    lines_ref, planes_ref, ratios_ref, _ = tables
    couples = points // 4
    last = 2 * couples - 1
    size = couples // groups
    steps = ratios_ref.shape[0] - 1
    first_half = lax.broadcasted_iota(jnp.int32, (points, LANES), 1) < points
    state = {"swept": jnp.zeros((points, LANES), jnp.float32)}

    def lines(group):
        even, odd = [], []
        for i in range(group * size, (group + 1) * size):
            near = load_left(i).astype(jnp.float32) * load_right(i).astype(jnp.float32)
            far = load_left(last - i).astype(jnp.float32) * load_right(last - i).astype(jnp.float32)
            even.append(jnp.where(first_half, near, far))
            odd.append(jnp.where(first_half, far, near))
        state["even", group] = sine_lines(jnp.concatenate(even, 0), lines_ref[0])
        state["odd", group] = sine_lines(jnp.concatenate(odd, 0), lines_ref[1])

    def planes(group):
        even, odd = state.pop(("even", group)), state.pop(("odd", group))
        for place in range(size):
            rows = slice(place * points, (place + 1) * points)
            value = jnp.concatenate([even[rows], odd[rows]], 1)
            state["modes", group * size + place] = sine_planes(value, planes_ref[...])

    def sweep(group):
        for i in range(group * size, (group + 1) * size):
            modes = state.pop(("modes", i))
            swept = (modes[:, :LANES] + state["swept"]) * ratios_ref[min(2 * i, steps)]
            put(2 * i, swept)
            swept = (modes[:, LANES:] + swept) * ratios_ref[min(2 * i + 1, steps)]
            put(2 * i + 1, swept)
            state["swept"] = swept

    return lines, planes, sweep


def backward_steps(get, give, tables, points, groups):
    lines_ref, planes_ref, ratios_ref, middle_ref = tables
    couples = points // 4
    last = 2 * couples - 1
    size = couples // groups
    steps = ratios_ref.shape[0] - 1
    first_half = lax.broadcasted_iota(jnp.int32, (points, LANES), 1) < points
    state = {}

    def members(group):
        return range(couples - 1 - group * size, couples - 1 - (group + 1) * size, -1)

    def solve(group):
        if group == 0:
            swept = get(last)
            state["solved"] = (swept + ratios_ref[min(last, steps)] * pltpu.roll(swept, points, 1)) * middle_ref[...]
        for i in members(group):
            if i < couples - 1:
                state["solved"] = get(2 * i + 1) + ratios_ref[min(2 * i + 1, steps)] * state["solved"]
            later = state["solved"]
            state["solved"] = get(2 * i) + ratios_ref[min(2 * i, steps)] * later
            state["modes", i] = jnp.concatenate([state["solved"], later], 1)

    def planes(group):
        for i in members(group):
            state["grid", i] = sine_planes(state.pop(("modes", i)), planes_ref[...])

    def lines(group):
        grids = [state.pop(("grid", i)) for i in members(group)]
        state["even", group] = sine_lines(jnp.concatenate([grid[:, :LANES] for grid in grids], 0), lines_ref[0])
        state["odd", group] = sine_lines(jnp.concatenate([grid[:, LANES:] for grid in grids], 0), lines_ref[1])

    def hand(group):
        even, odd = state.pop(("even", group)), state.pop(("odd", group))
        for place, i in enumerate(members(group)):
            rows = slice(place * points, (place + 1) * points)
            give(i, jnp.where(first_half, even[rows], odd[rows]))
            give(last - i, jnp.where(first_half, odd[rows], even[rows]))

    return solve, planes, lines, hand


def run_forward(steps):
    lines, planes, sweep = steps
    lines(0)
    planes(0)
    sweep(0)


def run_backward(steps):
    for step in steps:
        step(0)


def run_both(forward, backward, groups):
    lines, planes, sweep = forward
    solve, planes_back, lines_back, hand = backward
    for stage in range(groups + 3):
        if stage < groups:
            lines(stage)
            solve(stage)
        if 0 <= stage - 1 < groups:
            planes_back(stage - 1)
            planes(stage - 1)
        if 0 <= stage - 2 < groups:
            lines_back(stage - 2)
            sweep(stage - 2)
        if 0 <= stage - 3 < groups:
            hand(stage - 3)


def visit_kernel(firsts, lead_lists, fresh, with_own, streamed, points, *refs):
    refs = list(refs)
    offsets_ref = refs[0]
    lists_refs = refs[1 : 1 + lead_lists]
    own_ref = refs[1 + lead_lists]
    blocks = len(firsts)
    sources = refs[2 + lead_lists : 2 + lead_lists + blocks]
    at = 2 + lead_lists + blocks
    if not fresh:
        before_ref = refs[at]
        at += 1
    lines_hbm, planes_hbm, ratios_hbm, middle_hbm, totals = refs[at : at + 5]
    at += 5
    out_ref = totals
    if with_own:
        part_ref = refs[at]
        at += 1
    if streamed:
        totals, touched, load_sems, out_sems = refs[-4:]
        refs = refs[:-4]
    window, lines_ref, planes_ref, ratios_ref, middle_ref, kept, extra, items, starts, sems = refs[at:]
    own_count = own_ref.shape[0]
    slots = lists_refs[0].shape[0] - 1
    position = lax.rem(lax.axis_index("orb"), GROUP)

    sizes = [source.shape[0] for source in sources]
    bases = [own_count + sum(sizes[:slot]) for slot in range(blocks)]

    def brought(slot):
        place = window.at[pl.ds(bases[slot], sizes[slot])]
        return pltpu.make_async_copy(sources[slot], place, sems.at[slot + 1])

    own_copy = pltpu.make_async_copy(own_ref, window.at[pl.ds(0, own_count)], sems.at[0])
    own_copy.start()
    constants = [
        pltpu.make_async_copy(source, target, sems.at[blocks + 2 + at])
        for at, (source, target) in enumerate(
            ((lines_hbm, lines_ref), (planes_hbm, planes_ref), (ratios_hbm, ratios_ref), (middle_hbm, middle_ref))
        )
    ]
    for copy in constants:
        copy.start()
    for slot in range(blocks):
        brought(slot).start()
    if fresh:
        totals[...] = jnp.zeros_like(totals)
    elif not streamed:
        before = pltpu.make_async_copy(before_ref, totals, sems.at[blocks + 1])
        before.start()
    else:
        loads = [pltpu.make_async_copy(before_ref.at[k], totals.at[k], load_sems.at[k]) for k in range(own_count)]
        leaves = [pltpu.make_async_copy(totals.at[k], out_ref.at[k], out_sems.at[k]) for k in range(own_count)]
        for k in range(own_count):
            loads[k].start()
            touched[k] = 0

    def note(keep, filled, own, other):
        @pl.when(keep)
        def _():
            items[filled, 0] = own
            items[filled, 1] = other
            if streamed:
                touched[own] = 1

        return filled + keep.astype(jnp.int32)

    filled = jnp.int32(0)
    if with_own:
        own_list = lists_refs[0]

        def add_own(row, filled):
            keep = (row < own_list[slots, 0]) & (own_list[row, 1] < own_count)
            return note(keep, filled, own_list[row, 0], own_list[row, 1])

        filled = lax.fori_loop(0, slots, add_own, filled)
    for slot in range(blocks):
        offset = offsets_ref[position, slot]
        starts[slot] = filled
        for which, list_ref in enumerate(lists_refs):
            distance = offset if which == 0 else which
            active = offset > 0 if which == 0 else offset == -which
            live = jnp.where(active, list_ref[slots, 0], 0)

            def add_block(row, filled):
                lead = list_ref[row, 0]
                follow = list_ref[row, 1] - distance * own_count
                there = (follow if which == 0 else lead) - firsts[slot]
                keep = (follow >= 0) & (follow < own_count) & (there >= 0) & (there < sizes[slot])
                return note(keep, filled, lead if which == 0 else follow, bases[slot] + there)

            filled = lax.fori_loop(0, live, add_block, filled)

    own_copy.wait()
    if with_own:
        size = part_ref.shape[0]
        part_copy = pltpu.make_async_copy(window.at[pl.ds(own_count - size, size)], part_ref, sems.at[0])
        part_copy.start()
    for copy in constants:
        copy.wait()

    tables = (lines_ref, planes_ref, ratios_ref, middle_ref)

    def forward(item, groups):
        for slot in range(blocks):
            @pl.when(item == starts[slot])
            def _():
                brought(slot).wait()

        mine = items[item, 0]
        other = items[item, 1]
        side = lax.rem(item, 2)

        def put(index, swept):
            kept[side, index] = swept

        return forward_steps(
            lambda index: window[mine, :, tile(index)],
            lambda index: window[other, :, tile(index)],
            put, tables, points, groups,
        )

    def backward(item, groups):
        mine = items[item, 0]
        other = items[item, 1]
        side = lax.rem(item, 2)

        def give(index, potential):
            totals[mine, :, tile(index)] -= potential * window[other, :, tile(index)].astype(jnp.float32)
            if with_own:
                extra[:, tile(index)] = potential

        return backward_steps(lambda index: kept[side, index], give, tables, points, groups)

    def finish(item):
        if with_own:
            mine = items[item, 0]
            other = items[item, 1]

            @pl.when((other < own_count) & (other != mine))
            def _():
                def give_back(index, carried):
                    held = window[mine, :, tile(index)].astype(jnp.float32)
                    totals[other, :, tile(index)] -= extra[:, tile(index)] * held
                    return carried

                lax.fori_loop(0, points // 2, give_back, 0)

    @pl.when(filled > 0)
    def _():
        run_forward(forward(0, 1))

    if streamed:
        for k in range(own_count):
            loads[k].wait()

            @pl.when(touched[k] == 0)
            def _():
                leaves[k].start()
    elif not fresh:
        before.wait()

    def visit(item, carried):
        run_both(forward(item, GROUPS), backward(item - 1, GROUPS), GROUPS)
        finish(item - 1)
        return carried

    lax.fori_loop(1, filled, visit, 0)

    @pl.when(filled > 0)
    def _():
        run_backward(backward(filled - 1, 1))
        finish(filled - 1)

    if streamed:
        for k in range(own_count):
            @pl.when(touched[k] != 0)
            def _():
                leaves[k].start()
    for slot in range(blocks):
        @pl.when(starts[slot] == filled)
        def _():
            brought(slot).wait()
    if with_own:
        part_copy.wait()
    if streamed:
        for copy in leaves:
            copy.wait()


def visit_blocks(blocks, lists, own, before, constants, with_own=False, streamed=False):
    own_count, points, area = own.shape
    fresh = before is None
    place = pl.BlockSpec(memory_space=pl.ANY if streamed else pltpu.VMEM)
    total = jax.ShapeDtypeStruct(own.shape, jnp.float32)
    part = jax.ShapeDtypeStruct((own_count - max(own_count // 4, 1), points, area), own.dtype)
    most = (lists[0].shape[0] - 1) * (len(blocks) + 1)
    passed = [own, *(block[3] for block in blocks), *([] if fresh else [before]), *constants]
    return pl.pallas_call(
        functools.partial(visit_kernel, tuple(block[2] for block in blocks), len(lists), fresh, with_own, streamed, points),
        out_shape=[total, part] if with_own else total,
        in_specs=[pl.BlockSpec(memory_space=pltpu.SMEM)] * (1 + len(lists))
        + [pl.BlockSpec(memory_space=pl.ANY)] * len(passed),
        out_specs=[place, pl.BlockSpec(memory_space=pl.ANY)] if with_own else place,
        scratch_shapes=[
            pltpu.VMEM((own_count + sum(block[3].shape[0] for block in blocks), points, area), jnp.bfloat16),
            *[pltpu.VMEM(table.shape, table.dtype) for table in constants],
            pltpu.VMEM((2, points // 2, points, LANES), jnp.float32),
            pltpu.VMEM((points, area) if with_own else (8, LANES), jnp.float32),
            pltpu.SMEM((most, 2), jnp.int32),
            pltpu.SMEM((len(blocks),), jnp.int32),
            pltpu.SemaphoreType.DMA((len(blocks) + 2 + len(constants),)),
            *(
                [
                    pltpu.VMEM(own.shape, jnp.float32),
                    pltpu.SMEM((own_count,), jnp.int32),
                    pltpu.SemaphoreType.DMA((own_count,)),
                    pltpu.SemaphoreType.DMA((own_count,)),
                ]
                if streamed
                else []
            ),
        ],
        compiler_params=pltpu.CompilerParams(vmem_limit_bytes=VMEM_BYTES),
        cost_estimate=pl.CostEstimate(flops=0, bytes_accessed=0, transcendentals=0),
    )(jnp.asarray(offsets([block[:2] for block in blocks])), *lists, *passed)


def shards(orbitals, pair_list, pair_counts):
    count = lax.axis_size("orb")
    table = routes(count)
    constants = [jnp.asarray(t) for t in tables(orbitals.shape[1])]

    def send(value, name):
        return lax.ppermute(value, "orb", table[name])

    listed = jnp.concatenate([pair_list, jnp.broadcast_to(pair_counts[:, None], (1, 2))], 0)
    cut = max(orbitals.shape[0] // 4, 1)
    partner = send(orbitals, "core")
    lead = send(orbitals, "lead")
    early = send(orbitals[:cut], "rest")
    beside = send(listed, "core")
    later, partner = lax.optimization_barrier((listed, partner))
    behind = [
        lax.ppermute(later, "orb", [(d, (d + distance) % count) for d in range(count)])
        for distance in range(1, REACH + 1)
    ]
    totals, late = visit_blocks([("core", False, 0, partner)], [listed, beside], orbitals, None, constants, True)

    lead, early, late, totals, *behind = lax.optimization_barrier((lead, early, late, totals, *behind))
    lists = [listed] + behind
    handed = send(lead, "pass")
    lead_shared = send(lead, "lead_shared")
    early_shared = send(early, "rest_shared")
    blocks = [("lead", False, 0, lead), ("rest", False, 0, early)]
    blocks += [("lead", True, 0, lead_shared), ("rest", True, 0, early_shared)]
    totals = visit_blocks(blocks, lists, orbitals, totals, constants)

    late, handed, totals = lax.optimization_barrier((late, handed, totals))
    late = send(late, "rest")
    handed_shared = send(handed, "pass_shared")
    blocks = [("pass", False, 0, handed), ("pass", True, 0, handed_shared)]
    totals = visit_blocks(blocks, lists, orbitals, totals, constants)

    late, totals = lax.optimization_barrier((late, totals))
    late_shared = send(late, "rest_shared")
    totals = visit_blocks([("rest", False, cut, late)], lists, orbitals, totals, constants)
    return visit_blocks([("rest", True, cut, late_shared)], lists, orbitals, totals, constants, streamed=True)


def solution(mesh):
    return jax.shard_map(
        shards,
        mesh=mesh,
        in_specs=(P("orb", None, None), P("orb", None), P("orb")),
        out_specs=P("orb", None, None),
        check_vma=False,
    )
```
